768 devices in a mesh: dom: 192 (over y, z, core), sub: 4 (over x).
Axes of the slice: x: 4, y: 8, z: 12, core: 2. Of those that a mesh axis runs over, the one named last changes fastest.
Arguments:
- section_state: float32 [6144, 5, 128], P(('dom', 'sub')), may hold values from -2.5 to 10, as said below
- base_state: float32 [6144, 5, 128], P(('dom', 'sub')), may hold values from -2.5 to 10, as said below
- pseudo_interval_ratio: float32 [6144, 128], P(('dom', 'sub')), may hold values from 0.1 to 0.4
- send_list: int32 [192, 4, 4, 4], P('dom', 'sub'), may hold values from -1 to 7, as said below
- face_tiles: bfloat16 [24576, 3, 128, 128], P(('dom', 'sub')), may hold values from -0.15625 to 0.15625
- tile_row: int32 [24576], P(('dom', 'sub')), may hold values from 0 to 31, as said below
- tile_col: int32 [24576], P(('dom', 'sub')), may hold values from 0 to 95, as said below
- tile_flip: int32 [24576], P(('dom', 'sub')), may hold values 0 or 1
Outputs:
- updated_state: float32 [6144, 5, 128], P(('dom', 'sub'))
The draws below stay inside these ranges and needn't reach their ends.
Inputs may be any that keep to these rules, and one draw needn't show every extreme that they name: `send_list`: in each list the first entries (one to 4 of them) name distinct blocks of the sending device; the others are -1. One list of every partition has all 4 entries, and so does the list of every partition's last sub-partition for offset -2. `tile_row`: every block of a partition owns exactly 4 of the partition's tiles. `tile_col`: A tile's column is an own block of its partition (below 32) or a ghost slot whose sending partition exists on the curve (0 <= q < 192) and whose list entry is not -1. `section_state`: density and pressure lie in 0.5 to 2 in every cell; energy = pressure / 0.4 + 0.5 |momentum|^2 / density. `base_state`: density and pressure lie in 0.5 to 2 in every cell; energy = pressure / 0.4 + 0.5 |momentum|^2 / density.
All inputs are finite; a program needn't handle non-finite values. No bound on the sum of `tile_flip` on one device may be relied on, other than what follows from the above.
Results may differ from the reference program's by a relative error of at most 0.00042.
Values sent between devices are 32-bit elements; how exact they have to be, the bound alone decides.
A program may use at most 32 MiB of HBM per device.

```python
import math
import jax
import jax.numpy as jnp
from jax import lax

CELLS = 128
BLK_DEV = 8
TPB = 4
GSEND = 4
P_BLK = 32
GHOSTS = 64
NBLK = 6144
TILES = 24576
N_DOM = 192
N_SUB = 4


gamma_gas = 1.4


curve_steps = (1, -1, 2, -2)


def assemble(gas_rho_field, velocity, normal_load_field):
    energy = normal_load_field / (gamma_gas - 1.0) + 0.5 * gas_rho_field * jnp.sum(velocity * velocity, axis=1)
    return jnp.concatenate([gas_rho_field[:, None], gas_rho_field[:, None] * velocity, energy[:, None]], axis=1)


def positive_field(key):
    return jnp.exp(jax.random.uniform(key, (NBLK, CELLS), jnp.float32, math.log(0.5), math.log(2.0)))


def draw_section_state(key, part):
    key = jax.random.fold_in(key, 11)
    keys = jax.random.split(key, 3)
    gas_rho_field = positive_field(keys[0])
    normal_load_field = positive_field(keys[2])
    velocity = 0.4 * jnp.clip(jax.random.normal(keys[1], (NBLK, 3, CELLS), jnp.float32), -3.0, 3.0)
    return assemble(gas_rho_field, velocity, normal_load_field)


def draw_base_state(key, part):
    key = jax.random.fold_in(key, 12)
    keys = jax.random.split(key, 3)
    gas_rho_field = positive_field(keys[0])
    normal_load_field = positive_field(keys[2])
    velocity = 0.4 * jnp.clip(jax.random.normal(keys[1], (NBLK, 3, CELLS), jnp.float32), -3.0, 3.0)
    return assemble(gas_rho_field, velocity, normal_load_field)


def ghost_lists(key):
    counts = jax.random.randint(jax.random.fold_in(key, 101), (N_DOM, N_SUB, 4), 1, GSEND + 1)
    chosen = jax.random.randint(jax.random.fold_in(key, 102), (N_DOM,), 0, N_SUB * 4)
    flat = counts.reshape(N_DOM, N_SUB * 4)
    positions = jnp.arange(N_SUB * 4)[None, :]
    full_list = (positions == chosen[:, None]) | (positions == N_SUB * 4 - 1)
    flat = jnp.where(full_list, GSEND, flat)
    counts = flat.reshape(N_DOM, N_SUB, 4)
    scores = jax.random.randint(jax.random.fold_in(key, 103), (N_DOM, N_SUB, 4, BLK_DEV), 0, 2 ** 20) * BLK_DEV + jnp.arange(BLK_DEV)
    order = jnp.argsort(scores, axis=-1)[..., :GSEND]
    lists = jnp.where(jnp.arange(GSEND) < counts[..., None], order, -1)
    return (counts.astype(jnp.int32), lists.astype(jnp.int32))


def tile_layout(key):
    counts, lists = ghost_lists(key)
    per_region = TPB * P_BLK
    slots = jnp.arange(per_region, dtype=jnp.int32)
    regions = jnp.arange(N_DOM, dtype=jnp.int32)
    ghost_slot = jnp.minimum(slots, GHOSTS - 1)
    offset_pos = ghost_slot // (N_SUB * GSEND)
    sender_sub = ghost_slot // GSEND % N_SUB
    within = ghost_slot % GSEND
    shifts = jnp.array(curve_steps, dtype=jnp.int32)[offset_pos]
    sources = regions[:, None] - shifts[None, :]
    inside = (sources >= 0) & (sources < N_DOM)
    live_count = counts[sources % N_DOM, sender_sub[None, :], offset_pos[None, :]]
    live = inside & (within[None, :] < live_count) & (slots[None, :] < GHOSTS)
    random_cols = jax.random.randint(jax.random.fold_in(key, 201), (N_DOM, per_region), 0, P_BLK)
    columns = jnp.where(live, P_BLK + slots[None, :], random_cols)
    rows_all = jnp.broadcast_to(slots % P_BLK, (N_DOM, per_region))
    scores = jax.random.randint(jax.random.fold_in(key, 202), (N_DOM, per_region), 0, 2 ** 20) * per_region + slots[None, :]
    order = jnp.argsort(scores, axis=1)
    rows_all = jnp.take_along_axis(rows_all, order, axis=1)
    columns = jnp.take_along_axis(columns, order, axis=1)
    return (rows_all.reshape(-1).astype(jnp.int32), columns.reshape(-1).astype(jnp.int32))


def draw_send_list(key, part):
    result = ghost_lists(key)[1]
    return result


def draw_tile_row(key, part):
    result = tile_layout(key)[0]
    return result


def draw_tile_col(key, part):
    result = tile_layout(key)[1]
    return result


def set_ends(entries, key, least, largest):
    dims = entries.shape
    index_at = [jax.random.randint(jax.random.fold_in(key, axis), (), 0, dims[axis]) for axis in range(len(dims))]
    entries = entries.at[tuple(index_at)].set(least)
    longest = dims.index(max(dims))
    index_at[longest] = (index_at[longest] + 1) % dims[longest]
    return entries.at[tuple(index_at)].set(largest)


def levels(own_key, extent, pieces, smallest, top_value):
    factor_of, own = 1.0, jax.random.fold_in(own_key, 6)
    for axis_at, parts in pieces:
        draws = jnp.exp(jax.random.uniform(jax.random.fold_in(own, axis_at), (parts,), jnp.float32, smallest / len(pieces), top_value / len(pieces)))
        factor_of = factor_of * jnp.repeat(draws, extent[axis_at] // parts).reshape([-1 if axis == axis_at else 1 for axis in range(len(extent))])
    return factor_of


def centred(rng, extent, scale, limit, cuts=(), kind=jnp.bfloat16):
    gain = levels(rng, extent, cuts, -0.22, 0.18) if cuts else 1.0
    drawn = jax.random.normal(rng, extent, jnp.float32) * scale * gain
    return jnp.minimum(jnp.maximum(drawn, -limit), limit).astype(kind)


def setup_inputs(seed: int = 0) -> dict:
    key_list = jax.random.split(jax.random.key(seed), 9)
    return {
        "section_state": draw_section_state(jax.random.fold_in(key_list[8], 71), 0),
        "base_state": draw_base_state(jax.random.fold_in(key_list[8], 71), 0),
        "pseudo_interval_ratio": jnp.clip(jnp.exp(math.log(0.4) - 1.3862944 * jax.random.uniform(key_list[2], (NBLK, CELLS), jnp.float32) ** levels(key_list[2], (NBLK, CELLS), ((0, 768),), -0.2, 0.2)), 0.1, 0.4),
        "send_list": draw_send_list(jax.random.fold_in(key_list[8], 71), 0),
        "face_tiles": centred(key_list[4], (TILES, 3, CELLS, CELLS), (3 * CELLS * TPB) ** -0.5, 0.15625, ((0, 768),)),
        "tile_row": draw_tile_row(jax.random.fold_in(key_list[8], 71), 0),
        "tile_col": draw_tile_col(jax.random.fold_in(key_list[8], 71), 0),
        "tile_flip": set_ends((jax.random.randint(key_list[7], (TILES,), 0, 2) < 1).astype(jnp.int32), jax.random.fold_in(key_list[7], 1), 0, 1),
    }


gamma_gas = 1.4
viscosity = 0.3
conductivity = 1.46
smoothing = 0.1
section_coef = 0.5
curve_steps = (1, -1, 2, -2)

def primitives(conserved):
    gas_rho_field = conserved[:, 0]
    momentum = conserved[:, 1:4]
    velocity = momentum / gas_rho_field[:, None]
    normal_load_field = (gamma_gas - 1.0) * (conserved[:, 4] - 0.5 * lax.optimization_barrier(jnp.sum(momentum * velocity, axis=1)))
    return (gas_rho_field, velocity, normal_load_field)

def convective(conserved, velocity, normal_load_field):
    momentum = conserved[:, 1:4]
    identity = jnp.eye(3, dtype=jnp.float32)
    moment_flux = momentum[:, None, :, :] * velocity[:, :, None, :] + normal_load_field[:, None, None, :] * identity[None, :, :, None]
    energy_flux = (conserved[:, 4] + normal_load_field)[:, None, :] * velocity
    return jnp.concatenate([momentum[:, :, None, :], moment_flux, energy_flux[:, :, None, :]], axis=2)

def viscous(gas_rho_field, velocity, normal_load_field, received_gradient_rows):
    shear = received_gradient_rows[:, :, 1:4]
    divergence = shear[:, 0, 0] + shear[:, 1, 1] + shear[:, 2, 2]
    identity = jnp.eye(3, dtype=jnp.float32)
    stress = viscosity * (shear + jnp.swapaxes(shear, 1, 2) - 2.0 / 3.0 * divergence[:, None, None, :] * identity[None, :, :, None])
    heat_level_field = normal_load_field / gas_rho_field
    heat_gradient = (received_gradient_rows[:, :, 4] - heat_level_field[:, None, :] * received_gradient_rows[:, :, 0]) / gas_rho_field[:, None, :]
    work_flux = lax.optimization_barrier(jnp.sum(stress * velocity[:, None, :, :], axis=2)) + conductivity * heat_gradient
    starting_rho_field = jnp.zeros_like(work_flux)[:, :, None, :]
    return jnp.concatenate([starting_rho_field, stress, work_flux[:, :, None, :]], axis=2)

def wave_speed(gas_rho_field, velocity, normal_load_field):
    return jnp.sqrt(lax.optimization_barrier(jnp.sum(velocity * velocity, axis=1)) + gamma_gas * normal_load_field / gas_rho_field)

def oriented_tiles(face_tiles, tile_flip):
    return jnp.where(tile_flip[:, None, None, None] == 1, -jnp.swapaxes(face_tiles, 2, 3), face_tiles)

def extended(values_in, send_list, subdomain):
    owned = lax.dynamic_slice_in_dim(values_in, subdomain * P_BLK, P_BLK, 0)
    shifts = jnp.array(curve_steps, dtype=jnp.int32)
    sources = (subdomain - shifts) % N_DOM
    lists = send_list[sources][jnp.arange(4), :, jnp.arange(4)]
    source_regions = jnp.arange(N_SUB, dtype=jnp.int32)
    blocks_at = (sources[:, None, None] * N_SUB + source_regions[None, :, None]) * BLK_DEV + jnp.maximum(lists, 0)
    return jnp.concatenate([owned, values_in[blocks_at.reshape(-1)]], axis=0)

def reference(section_state, base_state, pseudo_interval_ratio, send_list, face_tiles, tile_row, tile_col, tile_flip):
    per_region = TPB * P_BLK

    def region_tiles(subdomain):
        start = subdomain * per_region
        tiles_here = lax.dynamic_slice_in_dim(face_tiles, start, per_region, 0)
        flips = lax.dynamic_slice_in_dim(tile_flip, start, per_region, 0)
        rows_here = lax.dynamic_slice_in_dim(tile_row, start, per_region, 0)
        cols_here = lax.dynamic_slice_in_dim(tile_col, start, per_region, 0)
        owners = (jnp.arange(P_BLK, dtype=jnp.int32)[:, None] == rows_here[None, :]).astype(jnp.float32)
        return (oriented_tiles(tiles_here, flips), owners, rows_here, cols_here)

    def region_slopes(subdomain):
        oriented, owners, rows_here, cols_here = region_tiles(subdomain)
        columns = extended(section_state, send_list, subdomain)[cols_here]
        gas_rho_field, velocity, normal_load_field = primitives(columns)
        prim_cols = jnp.concatenate([gas_rho_field[:, None], velocity, normal_load_field[:, None]], axis=1).astype(jnp.bfloat16)
        terms = jnp.einsum('tdab,tvb->tdva', oriented.astype(jnp.float32), prim_cols.astype(jnp.float32))
        summed = jnp.dot(owners, terms.reshape(per_region, -1), precision=lax.Precision.HIGHEST)
        return summed.reshape(P_BLK, 15, CELLS)
    slopes = lax.map(region_slopes, jnp.arange(N_DOM, dtype=jnp.int32)).reshape(NBLK, 15, CELLS)

    def region_residual(subdomain):
        oriented, owners, rows_here, cols_here = region_tiles(subdomain)
        ext_state = extended(section_state, send_list, subdomain)
        columns = ext_state[cols_here]
        row_state = ext_state[rows_here]
        col_slopes = extended(slopes, send_list, subdomain)[cols_here].reshape(per_region, 3, 5, CELLS)
        gas_rho_field, velocity, normal_load_field = primitives(columns)
        fluxes = (convective(columns, velocity, normal_load_field) - viscous(gas_rho_field, velocity, normal_load_field, col_slopes)).astype(jnp.bfloat16)
        scaled = (wave_speed(gas_rho_field, velocity, normal_load_field)[:, None, :] * columns).astype(jnp.bfloat16)
        row_density, row_velocity, row_pressure = primitives(row_state)
        row_scaled = wave_speed(row_density, row_velocity, row_pressure)[:, None, :] * row_state
        absolute = lax.optimization_barrier(jnp.sum(jnp.abs(oriented.astype(jnp.float32)), axis=1)).astype(jnp.bfloat16)
        flux_sum = jnp.einsum('tdab,tdvb->tva', oriented.astype(jnp.float32), fluxes.astype(jnp.float32))
        spread = jnp.einsum('tab,tvb->tva', absolute.astype(jnp.float32), scaled.astype(jnp.float32))
        spread = spread - lax.optimization_barrier(jnp.sum(absolute.astype(jnp.float32), axis=2))[:, None, :] * row_scaled
        contribution = flux_sum - smoothing * spread
        summed = jnp.dot(owners, contribution.reshape(per_region, -1), precision=lax.Precision.HIGHEST)
        return summed.reshape(P_BLK, 5, CELLS)
    residual = lax.map(region_residual, jnp.arange(N_DOM, dtype=jnp.int32)).reshape(NBLK, 5, CELLS)
    return base_state - section_coef * pseudo_interval_ratio[:, None, :] * residual
```

```python
import functools

import jax
import jax.numpy as jnp
from jax import lax
from jax.experimental import pallas as pl
from jax.experimental.pallas import tpu as pltpu
from jax.sharding import PartitionSpec as P

MESH = pl.DeviceIdType.MESH
F32, BF16 = jnp.float32, jnp.bfloat16
CURVE_STEPS = (1, -1, 2, -2)
SUBS = 4
OWN = 8
PART = SUBS * OWN
LIST = 4
TILES = 32
CELLS = 128
SLOTS = PART + len(CURVE_STEPS) * SUBS * LIST
ROWS = 8
CHUNKS = 4
NUM_V = 8
NUM_R = 6


def row_sums(owners, parts):
    x = jnp.concatenate(parts, axis=1)
    high = x.astype(BF16)
    rest = x - high.astype(F32)
    mid = rest.astype(BF16)
    low = (rest - mid.astype(F32)).astype(BF16)
    total = jnp.dot(
        owners, jnp.concatenate([high, mid, low], axis=0), preferred_element_type=F32
    )
    return [total[:, i * CELLS : (i + 1) * CELLS] for i in range(len(parts))]


def kernel(
    doms,
    state_h,
    base_h,
    ratio_h,
    send_s,
    row_s,
    col_s,
    flip_s,
    tiles_h,
    out_ref,
    raw,
    weights,
    absolute,
    state,
    base,
    ratio,
    own,
    packets,
    ext,
    gathered,
    terms,
    part_v,
    recv_v,
    mixed,
    own_v,
    packets_v,
    ext_v,
    gathered_v,
    scaled,
    spread,
    fluxes,
    contribution,
    part_r,
    recv_r,
    tile_sem,
    load_sem,
    send_sem,
    recv_sem,
):
    me, sub = lax.axis_index("dom"), lax.axis_index("sub")
    peers = [lax.rem(sub + i, SUBS) for i in range(1, SUBS)]
    targets = [lax.rem(me + (step + doms), doms) for step in CURVE_STEPS]

    barrier = pltpu.get_barrier_semaphore()
    for peer in peers:
        pl.semaphore_signal(barrier, inc=1, device_id=(me, peer), device_id_type=MESH)
    for target in targets:
        for s in range(SUBS):
            pl.semaphore_signal(
                barrier, inc=1, device_id=(target, jnp.int32(s)), device_id_type=MESH
            )

    loads = [
        pltpu.make_async_copy(state_h, state, load_sem.at[0]),
        pltpu.make_async_copy(base_h, base, load_sem.at[1]),
        pltpu.make_async_copy(ratio_h, ratio, load_sem.at[2]),
    ]
    for load in loads:
        load.start()
    per_chunk = TILES // CHUNKS
    tile_loads = [
        pltpu.make_async_copy(
            tiles_h.at[pl.ds(c * per_chunk, per_chunk)],
            raw.at[pl.ds(c * per_chunk, per_chunk)],
            tile_sem.at[c],
        )
        for c in range(CHUNKS)
    ]
    for load in tile_loads:
        load.start()

    def remote(source, target, number, device):
        pltpu.make_async_remote_copy(
            src_ref=source,
            dst_ref=target,
            send_sem=send_sem.at[number],
            recv_sem=recv_sem.at[number],
            device_id=device,
            device_id_type=MESH,
        ).start()

    def drain(sems, number, like):
        pltpu.make_async_copy(like, like, sems.at[number]).wait()

    def share(values, lists, extended, number):
        at = sub * OWN
        for k in range(len(CURVE_STEPS)):
            slot = PART + (k * SUBS + sub) * LIST
            for s in range(SUBS):
                remote(
                    lists.at[pl.ds(k * LIST, LIST)],
                    extended.at[pl.ds(slot, LIST)],
                    number,
                    (targets[k], jnp.int32(s)),
                )
        for peer in peers:
            remote(values, extended.at[pl.ds(at, OWN)], number, (me, peer))
        extended[pl.ds(at, OWN)] = values[...]

    shared = SLOTS - OWN
    flat = lambda ref: ref.reshape(ref.shape[0] * ROWS, CELLS)

    def pick(values, lists):
        for k in range(len(CURVE_STEPS)):
            for j in range(LIST):
                lists[k * LIST + j] = values[jnp.maximum(send_s[0, 0, k, j], 0)]

    loads[0].wait()
    density, energy = state[0], state[4]
    momentum = [state[1 + i] for i in range(3)]
    velocity = [m / density for m in momentum]
    pressure = 0.4 * (
        energy
        - 0.5
        * (momentum[0] * velocity[0] + momentum[1] * velocity[1] + momentum[2] * velocity[2])
    )
    square = velocity[0] * velocity[0] + velocity[1] * velocity[1] + velocity[2] * velocity[2]
    speed = jnp.sqrt(square + 1.4 * pressure / density)
    for i, value in enumerate(
        [density, *velocity, pressure, energy, speed, jnp.zeros_like(speed)]
    ):
        flat(own)[pl.ds(i, OWN, stride=ROWS), :] = value
    pick(own, packets)

    pl.semaphore_wait(barrier, SUBS - 1 + len(CURVE_STEPS) * SUBS)
    share(own, packets, ext, 0)

    lane = lax.broadcasted_iota(jnp.int32, (PART, 3 * TILES), 1)
    lane = lax.rem(lane, TILES)
    tile_rows = jnp.zeros((PART, 3 * TILES), jnp.int32)
    for t in range(TILES):
        tile_rows = jnp.where(lane == t, row_s[t], tile_rows)
    block_row = lax.broadcasted_iota(jnp.int32, (PART, 3 * TILES), 0)
    owners = jnp.where(block_row == tile_rows, 1.0, 0.0).astype(BF16)

    def orient(t, carry):
        flipped = jnp.full((CELLS, CELLS), flip_s[t], jnp.int32) == 1
        total = None
        for d in range(3):
            tile = raw[t, d].astype(F32)
            tile = jnp.where(flipped, -tile, tile.T)
            weights[t, pl.ds(d * CELLS, CELLS), :] = tile.astype(BF16)
            total = jnp.abs(tile) if total is None else total + jnp.abs(tile)
        absolute[t] = total.astype(BF16)
        return carry

    for c in range(CHUNKS):
        tile_loads[c].wait()
        lax.fori_loop(c * per_chunk, (c + 1) * per_chunk, orient, 0)
    ones = jnp.ones((TILES, CELLS), F32)
    scaled[pl.ds(5 * TILES, TILES), :] = ones
    for v in (6, 7):
        scaled[pl.ds(v * TILES, TILES), :] = jnp.zeros_like(ones)
    for d in range(3):
        for v in (5, 6, 7):
            fluxes[pl.ds((d * ROWS + v) * TILES, TILES), :] = jnp.zeros_like(ones)

    drain(recv_sem, 0, ext.at[pl.ds(0, shared)])

    def slope(t, carry):
        at = pl.multiple_of(t * ROWS, ROWS)
        column = ext[col_s[t]]
        gathered[pl.ds(at, ROWS), :] = column
        column = column.astype(BF16)
        for d in range(3):
            terms[pl.ds(pl.multiple_of((t * 3 + d) * ROWS, ROWS), ROWS), :] = jnp.dot(
                column, weights[t, pl.ds(d * CELLS, CELLS), :], preferred_element_type=F32
            )
        return carry

    lax.fori_loop(0, TILES, slope, 0, unroll=4)

    def term(d, v):
        return terms[pl.ds(d * ROWS + v, TILES, stride=3 * ROWS), :]

    shear = [[term(d, 1 + i) for i in range(3)] for d in range(3)]
    third = (2.0 / 3.0) * (shear[0][0] + shear[1][1] + shear[2][2])
    sums = row_sums(
        owners,
        [
            2.0 * shear[0][0] - third,
            2.0 * shear[1][1] - third,
            shear[0][1] + shear[1][0],
            shear[0][2] + shear[2][0],
            shear[1][2] + shear[2][1],
        ]
        + [term(d, 4) for d in range(3)]
        + [term(d, 0) for d in range(3)],
    )
    rho, v0, v1, v2, press = [flat(ext)[pl.ds(v, PART, stride=ROWS), :] for v in range(5)]
    s00, s11, s01, s02, s12 = [0.3 * s for s in sums[:5]]
    s22 = -(s00 + s11)
    level = press / rho
    heat = [1.46 * (sums[5 + d] - level * sums[8 + d]) / rho for d in range(3)]
    work = [
        s00 * v0 + s01 * v1 + s02 * v2 + heat[0],
        s01 * v0 + s11 * v1 + s12 * v2 + heat[1],
        s02 * v0 + s12 * v1 + s22 * v2 + heat[2],
    ]
    for c, value in enumerate([s00, s11, s01, s02, s12, *work]):
        for s in range(SUBS):
            part_v[pl.ds((s * NUM_V + c) * OWN, OWN), :] = value[s * OWN : (s + 1) * OWN]

    def reduce_to_owners(part, recv, count, number):
        size = count * OWN
        for i, peer in enumerate(peers):
            remote(
                part.at[pl.ds(pl.multiple_of(peer * size, size), size)],
                recv.at[pl.ds(i * size, size)],
                number,
                (me, peer),
            )

    def reduced(part, recv, count, number):
        size = count * OWN
        drain(recv_sem, number, recv)
        total = part[pl.ds(pl.multiple_of(sub * size, size), size), :]
        for i in range(SUBS - 1):
            total = total + recv[pl.ds(i * size, size), :]
        return total

    reduce_to_owners(part_v, recv_v, NUM_V, 1)

    rho, v0, v1, v2, press, ener, wave = [
        gathered[pl.ds(v, TILES, stride=ROWS), :] for v in range(7)
    ]
    vel = [v0, v1, v2]
    mom = [rho * v for v in vel]
    for v, value in enumerate([rho, *mom, ener]):
        scaled[pl.ds(v * TILES, TILES), :] = wave * value

    def dissipate(t, carry):
        left = scaled[pl.ds(t, ROWS, stride=TILES), :].astype(BF16)
        spread[pl.ds(pl.multiple_of(t * ROWS, ROWS), ROWS), :] = jnp.dot(
            left, absolute[t], preferred_element_type=F32
        )
        return carry

    lax.fori_loop(0, TILES, dissipate, 0, unroll=4)

    mixed[...] = reduced(part_v, recv_v, NUM_V, 1)
    for r in range(OWN):
        own_v[r] = mixed[pl.ds(r, ROWS, stride=OWN), :]
    pick(own_v, packets_v)
    share(own_v, packets_v, ext_v, 2)
    drain(recv_sem, 2, ext_v.at[pl.ds(0, shared)])

    def gather_v(t, carry):
        gathered_v[pl.ds(pl.multiple_of(t * ROWS, ROWS), ROWS), :] = ext_v[col_s[t]]
        return carry

    lax.fori_loop(0, TILES, gather_v, 0, unroll=8)
    s00, s11, s01, s02, s12, w0, w1, w2 = [
        gathered_v[pl.ds(c, TILES, stride=ROWS), :] for c in range(NUM_V)
    ]
    stress = [[s00, s01, s02], [s01, s11, s12], [s02, s12, -(s00 + s11)]]
    work = [w0, w1, w2]
    for d in range(3):
        values = [mom[d]]
        for i in range(3):
            flow = mom[i] * vel[d]
            if i == d:
                flow = flow + press
            values.append(flow - stress[d][i])
        values.append((ener + press) * vel[d] - work[d])
        for v, value in enumerate(values):
            fluxes[pl.ds((d * ROWS + v) * TILES, TILES), :] = value

    def flux(t, carry):
        at = pl.multiple_of(t * ROWS, ROWS)
        left = jnp.concatenate(
            [fluxes[pl.ds(d * ROWS * TILES + t, ROWS, stride=TILES), :] for d in range(3)],
            axis=1,
        ).astype(BF16)
        total = jnp.dot(left, weights[t], preferred_element_type=F32)
        contribution[pl.ds(at, ROWS), :] = total - 0.1 * spread[pl.ds(at, ROWS), :]
        return carry

    lax.fori_loop(0, TILES, flux, 0, unroll=4)

    sums = row_sums(
        owners, [contribution[pl.ds(v, TILES, stride=ROWS), :] for v in range(NUM_R)]
    )
    for c, value in enumerate(sums):
        for s in range(SUBS):
            part_r[pl.ds((s * NUM_R + c) * OWN, OWN), :] = value[s * OWN : (s + 1) * OWN]
    reduce_to_owners(part_r, recv_r, NUM_R, 3)

    loads[1].wait()
    loads[2].wait()
    total = reduced(part_r, recv_r, NUM_R, 3)
    absolute_sum = total[5 * OWN : 6 * OWN] * speed
    half = 0.5 * ratio[...]
    for v, value in enumerate([density, *momentum, energy]):
        residual = total[v * OWN : (v + 1) * OWN] - absolute_sum * value
        out_ref[v] = base[v] - half * residual

    drain(send_sem, 0, ext.at[pl.ds(0, shared)])
    drain(send_sem, 1, recv_v)
    drain(send_sem, 2, ext_v.at[pl.ds(0, shared)])
    drain(send_sem, 3, recv_r)


def per_device(
    section_state, base_state, ratio, send_list, face_tiles, tile_row, tile_col, tile_flip
):
    any_space = pl.BlockSpec(memory_space=pl.ANY)
    smem = pl.BlockSpec(memory_space=pltpu.SMEM)
    blocks = lambda count: pltpu.VMEM((count, ROWS, CELLS), F32)
    row = lambda count: pltpu.VMEM((count, CELLS), F32)
    updated = pl.pallas_call(
        functools.partial(kernel, lax.axis_size("dom")),
        out_shape=jax.ShapeDtypeStruct((5, OWN, CELLS), F32),
        in_specs=[any_space] * 3 + [smem] * 4 + [any_space],
        out_specs=pl.BlockSpec(memory_space=pltpu.VMEM),
        scratch_shapes=[
            pltpu.VMEM((TILES, 3, CELLS, CELLS), BF16),
            pltpu.VMEM((TILES, 3 * CELLS, CELLS), BF16),
            pltpu.VMEM((TILES, CELLS, CELLS), BF16),
            pltpu.VMEM((5, OWN, CELLS), F32),
            pltpu.VMEM((5, OWN, CELLS), F32),
            pltpu.VMEM((OWN, CELLS), F32),
            blocks(OWN),
            blocks(len(CURVE_STEPS) * LIST),
            blocks(SLOTS),
            row(TILES * ROWS),
            row(TILES * 3 * ROWS),
            row(SUBS * NUM_V * OWN),
            row((SUBS - 1) * NUM_V * OWN),
            row(NUM_V * OWN),
            blocks(OWN),
            blocks(len(CURVE_STEPS) * LIST),
            blocks(SLOTS),
            row(TILES * ROWS),
            row(ROWS * TILES),
            row(TILES * ROWS),
            row(3 * ROWS * TILES),
            row(TILES * ROWS),
            row(SUBS * NUM_R * OWN),
            row((SUBS - 1) * NUM_R * OWN),
            pltpu.SemaphoreType.DMA((CHUNKS,)),
            pltpu.SemaphoreType.DMA((3,)),
            pltpu.SemaphoreType.DMA((4,)),
            pltpu.SemaphoreType.DMA((4,)),
        ],
        compiler_params=pltpu.CompilerParams(
            collective_id=0, has_side_effects=True, vmem_limit_bytes=60 * 1024 * 1024
        ),
    )(
        jnp.transpose(section_state, (1, 0, 2)),
        jnp.transpose(base_state, (1, 0, 2)),
        ratio,
        send_list,
        tile_row,
        tile_col,
        tile_flip,
        face_tiles,
    )
    return jnp.transpose(updated, (1, 0, 2))


def solution(mesh):
    return jax.shard_map(
        per_device,
        mesh=mesh,
        in_specs=(
            P(("dom", "sub"), None, None),
            P(("dom", "sub"), None, None),
            P(("dom", "sub"), None),
            P("dom", "sub", None, None),
            P(("dom", "sub"), None, None, None),
            P(("dom", "sub")),
            P(("dom", "sub")),
            P(("dom", "sub")),
        ),
        out_specs=P(("dom", "sub"), None, None),
        check_vma=False,
    )
```

```python
import functools

import jax
import jax.numpy as jnp
from jax import lax
from jax.experimental import pallas as pl
from jax.experimental.pallas import tpu as pltpu
from jax.sharding import PartitionSpec as P

MESH = pl.DeviceIdType.MESH
F32, BF16 = jnp.float32, jnp.bfloat16
CURVE_STEPS = (1, -1, 2, -2)
SUBS = 4
OWN = 8
PART = SUBS * OWN
LIST = 4
TILES = 32
CELLS = 128
SLOTS = PART + len(CURVE_STEPS) * SUBS * LIST
ROWS = 8
CHUNKS = 4
NUM_V = 8
NUM_R = 6


def row_sums(owners, parts):
    x = jnp.concatenate(parts, axis=1)
    high = x.astype(BF16)
    rest = x - high.astype(F32)
    mid = rest.astype(BF16)
    low = (rest - mid.astype(F32)).astype(BF16)
    total = jnp.dot(
        owners, jnp.concatenate([high, mid, low], axis=0), preferred_element_type=F32
    )
    return [total[:, i * CELLS : (i + 1) * CELLS] for i in range(len(parts))]


def kernel(
    doms,
    state_h,
    base_h,
    ratio_h,
    send_h,
    row_h,
    col_h,
    flip_h,
    tiles_h,
    out_ref,
    raw,
    weights,
    absolute,
    state,
    base,
    ratio,
    own,
    packets,
    ext,
    gathered,
    terms,
    part_v,
    recv_v,
    mixed,
    own_v,
    packets_v,
    ext_v,
    gathered_v,
    scaled,
    spread,
    fluxes,
    contribution,
    part_r,
    recv_r,
    send_s,
    row_s,
    col_s,
    flip_s,
    tile_sem,
    load_sem,
    send_sem,
    recv_sem,
):
    me, sub = lax.axis_index("dom"), lax.axis_index("sub")
    peers = [lax.rem(sub + i, SUBS) for i in range(1, SUBS)]
    targets = [me + step for step in CURVE_STEPS]
    inside = lambda dom: (dom >= 0) & (dom < doms)

    barrier = pltpu.get_barrier_semaphore()
    for peer in peers:
        pl.semaphore_signal(barrier, inc=1, device_id=(me, peer), device_id_type=MESH)
    greeted = SUBS - 1
    for target in targets:
        greeted = greeted + jnp.where(inside(target), SUBS, 0)

        @pl.when(inside(target))
        def _():
            for s in range(SUBS):
                pl.semaphore_signal(
                    barrier, inc=1, device_id=(target, jnp.int32(s)), device_id_type=MESH
                )


    loads = [
        pltpu.make_async_copy(state_h, state, load_sem.at[0]),
        pltpu.make_async_copy(base_h, base, load_sem.at[1]),
        pltpu.make_async_copy(ratio_h, ratio, load_sem.at[2]),
        pltpu.make_async_copy(send_h, send_s, load_sem.at[3]),
        pltpu.make_async_copy(row_h, row_s, load_sem.at[4]),
        pltpu.make_async_copy(col_h, col_s, load_sem.at[5]),
        pltpu.make_async_copy(flip_h, flip_s, load_sem.at[6]),
    ]
    for load in loads:
        load.start()
    per_chunk = TILES // CHUNKS
    tile_loads = [
        pltpu.make_async_copy(
            tiles_h.at[pl.ds(c * per_chunk, per_chunk)],
            raw.at[pl.ds(c * per_chunk, per_chunk)],
            tile_sem.at[c],
        )
        for c in range(CHUNKS)
    ]
    for load in tile_loads:
        load.start()

    def remote(source, target, number, device):
        pltpu.make_async_remote_copy(
            src_ref=source,
            dst_ref=target,
            send_sem=send_sem.at[number],
            recv_sem=recv_sem.at[number],
            device_id=device,
            device_id_type=MESH,
        ).start()

    def drain(sems, number, like):
        pltpu.make_async_copy(like, like, sems.at[number]).wait()

    def share(values, lists, extended, rows, first):
        at = sub * OWN
        for k in (2, 3, 1, 0):
            slot = PART + (k * SUBS + sub) * LIST

            @pl.when(inside(targets[k]))
            def _():
                for i in (2, 1, 3, 0):
                    remote(
                        lists.at[pl.ds(k * LIST, LIST), pl.ds(0, rows)],
                        extended.at[pl.ds(slot, LIST), pl.ds(0, rows)],
                        first + k,
                        (targets[k], lax.rem(sub + i, SUBS)),
                    )

        for peer in peers:
            remote(
                values.at[:, pl.ds(0, rows)],
                extended.at[pl.ds(at, OWN), pl.ds(0, rows)],
                first + 4,
                (me, peer),
            )
        extended[pl.ds(at, OWN)] = values[...]

    def shared(sems, extended, rows, first, sign):
        for k, step in enumerate(CURVE_STEPS):

            @pl.when(inside(me + sign * step))
            def _():
                drain(sems, first + k, extended.at[pl.ds(0, SUBS * LIST), pl.ds(0, rows)])

        drain(sems, first + 4, extended.at[pl.ds(0, PART - OWN), pl.ds(0, rows)])

    flat = lambda ref: ref.reshape(ref.shape[0] * ROWS, CELLS)

    def pick(values, lists):
        for k in range(len(CURVE_STEPS)):
            for j in range(LIST):
                lists[k * LIST + j] = values[jnp.maximum(send_s[0, 0, k, j], 0)]

    loads[0].wait()
    loads[3].wait()
    density, energy = state[0], state[4]
    momentum = [state[1 + i] for i in range(3)]
    velocity = [m / density for m in momentum]
    pressure = 0.4 * (
        energy
        - 0.5
        * (momentum[0] * velocity[0] + momentum[1] * velocity[1] + momentum[2] * velocity[2])
    )
    square = velocity[0] * velocity[0] + velocity[1] * velocity[1] + velocity[2] * velocity[2]
    speed = jnp.sqrt(square + 1.4 * pressure / density)
    for i, value in enumerate(
        [density, *velocity, pressure]
    ):
        flat(own)[pl.ds(i, OWN, stride=ROWS), :] = value
    pick(own, packets)

    pl.semaphore_wait(barrier, greeted)
    share(own, packets, ext, 5, 0)

    for load in loads[4:]:
        load.wait()
    lane = lax.broadcasted_iota(jnp.int32, (PART, 3 * TILES), 1)
    lane = lax.rem(lane, TILES)
    tile_rows = jnp.zeros((PART, 3 * TILES), jnp.int32)
    for t in range(TILES):
        tile_rows = jnp.where(lane == t, row_s[t], tile_rows)
    block_row = lax.broadcasted_iota(jnp.int32, (PART, 3 * TILES), 0)
    owners = jnp.where(block_row == tile_rows, 1.0, 0.0).astype(BF16)

    def orient(t, carry):
        flipped = jnp.full((CELLS, CELLS), flip_s[t], jnp.int32) == 1
        total = None
        for d in range(3):
            tile = raw[t, d].astype(F32)
            tile = jnp.where(flipped, -tile, tile.T)
            weights[t, pl.ds(d * CELLS, CELLS), :] = tile.astype(BF16)
            total = jnp.abs(tile) if total is None else total + jnp.abs(tile)
        absolute[t] = total.astype(BF16)
        return carry

    for c in range(CHUNKS):
        tile_loads[c].wait()
        lax.fori_loop(c * per_chunk, (c + 1) * per_chunk, orient, 0)
    ones = jnp.ones((TILES, CELLS), F32)
    scaled[pl.ds(5 * TILES, TILES), :] = ones
    for v in (6, 7):
        scaled[pl.ds(v * TILES, TILES), :] = jnp.zeros_like(ones)
    for d in range(3):
        for v in (5, 6, 7):
            fluxes[pl.ds((d * ROWS + v) * TILES, TILES), :] = jnp.zeros_like(ones)

    shared(recv_sem, ext, 5, 0, -1)

    def slope(t, carry):
        at = pl.multiple_of(t * ROWS, ROWS)
        column = ext[col_s[t]]
        gathered[pl.ds(at, ROWS), :] = column
        column = column.astype(BF16)
        for d in range(3):
            terms[pl.ds(pl.multiple_of((t * 3 + d) * ROWS, ROWS), ROWS), :] = jnp.dot(
                column, weights[t, pl.ds(d * CELLS, CELLS), :], preferred_element_type=F32
            )
        return carry

    lax.fori_loop(0, TILES, slope, 0, unroll=TILES)

    def term(d, v):
        return terms[pl.ds(d * ROWS + v, TILES, stride=3 * ROWS), :]

    shear = [[term(d, 1 + i) for i in range(3)] for d in range(3)]
    third = (2.0 / 3.0) * (shear[0][0] + shear[1][1] + shear[2][2])
    sums = row_sums(
        owners,
        [
            2.0 * shear[0][0] - third,
            2.0 * shear[1][1] - third,
            shear[0][1] + shear[1][0],
            shear[0][2] + shear[2][0],
            shear[1][2] + shear[2][1],
        ]
        + [term(d, 4) for d in range(3)]
        + [term(d, 0) for d in range(3)],
    )
    rho, v0, v1, v2, press = [flat(ext)[pl.ds(v, PART, stride=ROWS), :] for v in range(5)]
    s00, s11, s01, s02, s12 = [0.3 * s for s in sums[:5]]
    s22 = -(s00 + s11)
    level = press / rho
    heat = [1.46 * (sums[5 + d] - level * sums[8 + d]) / rho for d in range(3)]
    work = [
        s00 * v0 + s01 * v1 + s02 * v2 + heat[0],
        s01 * v0 + s11 * v1 + s12 * v2 + heat[1],
        s02 * v0 + s12 * v1 + s22 * v2 + heat[2],
    ]
    for c, value in enumerate([s00, s11, s01, s02, s12, *work]):
        for s in range(SUBS):
            part_v[pl.ds((s * NUM_V + c) * OWN, OWN), :] = value[s * OWN : (s + 1) * OWN]

    def reduce_to_owners(part, recv, count, number):
        size = count * OWN
        for i, peer in enumerate(peers):
            remote(
                part.at[pl.ds(pl.multiple_of(peer * size, size), size)],
                recv.at[pl.ds(i * size, size)],
                number,
                (me, peer),
            )

    def reduced(part, recv, count, number):
        size = count * OWN
        drain(recv_sem, number, recv)
        total = part[pl.ds(pl.multiple_of(sub * size, size), size), :]
        for i in range(SUBS - 1):
            total = total + recv[pl.ds(i * size, size), :]
        return total

    reduce_to_owners(part_v, recv_v, NUM_V, 10)

    rho, v0, v1, v2, press = [gathered[pl.ds(v, TILES, stride=ROWS), :] for v in range(5)]
    vel = [v0, v1, v2]
    square = v0 * v0 + v1 * v1 + v2 * v2
    ener = 2.5 * press + 0.5 * rho * square
    wave = jnp.sqrt(square + 1.4 * press / rho)
    mom = [rho * v for v in vel]
    for v, value in enumerate([rho, *mom, ener]):
        scaled[pl.ds(v * TILES, TILES), :] = wave * value

    def dissipate(t, carry):
        left = scaled[pl.ds(t, ROWS, stride=TILES), :].astype(BF16)
        spread[pl.ds(pl.multiple_of(t * ROWS, ROWS), ROWS), :] = jnp.dot(
            left, absolute[t], preferred_element_type=F32
        )
        return carry

    lax.fori_loop(0, TILES, dissipate, 0, unroll=TILES)

    mixed[...] = reduced(part_v, recv_v, NUM_V, 10)
    for r in range(OWN):
        own_v[r] = mixed[pl.ds(r, ROWS, stride=OWN), :]
    pick(own_v, packets_v)
    share(own_v, packets_v, ext_v, ROWS, 5)
    shared(recv_sem, ext_v, ROWS, 5, -1)

    def gather_v(t, carry):
        gathered_v[pl.ds(pl.multiple_of(t * ROWS, ROWS), ROWS), :] = ext_v[col_s[t]]
        return carry

    lax.fori_loop(0, TILES, gather_v, 0, unroll=TILES)
    s00, s11, s01, s02, s12, w0, w1, w2 = [
        gathered_v[pl.ds(c, TILES, stride=ROWS), :] for c in range(NUM_V)
    ]
    stress = [[s00, s01, s02], [s01, s11, s12], [s02, s12, -(s00 + s11)]]
    work = [w0, w1, w2]
    for d in range(3):
        values = [mom[d]]
        for i in range(3):
            flow = mom[i] * vel[d]
            if i == d:
                flow = flow + press
            values.append(flow - stress[d][i])
        values.append((ener + press) * vel[d] - work[d])
        for v, value in enumerate(values):
            fluxes[pl.ds((d * ROWS + v) * TILES, TILES), :] = value

    def flux(t, carry):
        at = pl.multiple_of(t * ROWS, ROWS)
        left = jnp.concatenate(
            [fluxes[pl.ds(d * ROWS * TILES + t, ROWS, stride=TILES), :] for d in range(3)],
            axis=1,
        ).astype(BF16)
        total = jnp.dot(left, weights[t], preferred_element_type=F32)
        contribution[pl.ds(at, ROWS), :] = total - 0.1 * spread[pl.ds(at, ROWS), :]
        return carry

    lax.fori_loop(0, TILES, flux, 0, unroll=TILES)

    sums = row_sums(
        owners, [contribution[pl.ds(v, TILES, stride=ROWS), :] for v in range(NUM_R)]
    )
    for c, value in enumerate(sums):
        for s in range(SUBS):
            part_r[pl.ds((s * NUM_R + c) * OWN, OWN), :] = value[s * OWN : (s + 1) * OWN]
    reduce_to_owners(part_r, recv_r, NUM_R, 11)

    loads[1].wait()
    loads[2].wait()
    total = reduced(part_r, recv_r, NUM_R, 11)
    absolute_sum = total[5 * OWN : 6 * OWN] * speed
    half = 0.5 * ratio[...]
    for v, value in enumerate([density, *momentum, energy]):
        residual = total[v * OWN : (v + 1) * OWN] - absolute_sum * value
        out_ref[v] = base[v] - half * residual

    shared(send_sem, ext, 5, 0, 1)
    drain(send_sem, 10, recv_v)
    shared(send_sem, ext_v, ROWS, 5, 1)
    drain(send_sem, 11, recv_r)


def per_device(
    section_state, base_state, ratio, send_list, face_tiles, tile_row, tile_col, tile_flip
):
    any_space = pl.BlockSpec(memory_space=pl.ANY)
    scalars = lambda *shape: pltpu.SMEM(shape, jnp.int32)
    blocks = lambda count: pltpu.VMEM((count, ROWS, CELLS), F32)
    row = lambda count: pltpu.VMEM((count, CELLS), F32)
    updated = pl.pallas_call(
        functools.partial(kernel, lax.axis_size("dom")),
        out_shape=jax.ShapeDtypeStruct((5, OWN, CELLS), F32),
        in_specs=[any_space] * 8,
        out_specs=pl.BlockSpec(memory_space=pltpu.VMEM),
        scratch_shapes=[
            pltpu.VMEM((TILES, 3, CELLS, CELLS), BF16),
            pltpu.VMEM((TILES, 3 * CELLS, CELLS), BF16),
            pltpu.VMEM((TILES, CELLS, CELLS), BF16),
            pltpu.VMEM((5, OWN, CELLS), F32),
            pltpu.VMEM((5, OWN, CELLS), F32),
            pltpu.VMEM((OWN, CELLS), F32),
            blocks(OWN),
            blocks(len(CURVE_STEPS) * LIST),
            blocks(SLOTS),
            row(TILES * ROWS),
            row(TILES * 3 * ROWS),
            row(SUBS * NUM_V * OWN),
            row((SUBS - 1) * NUM_V * OWN),
            row(NUM_V * OWN),
            blocks(OWN),
            blocks(len(CURVE_STEPS) * LIST),
            blocks(SLOTS),
            row(TILES * ROWS),
            row(ROWS * TILES),
            row(TILES * ROWS),
            row(3 * ROWS * TILES),
            row(TILES * ROWS),
            row(SUBS * NUM_R * OWN),
            row((SUBS - 1) * NUM_R * OWN),
            scalars(*send_list.shape),
            scalars(TILES),
            scalars(TILES),
            scalars(TILES),
            pltpu.SemaphoreType.DMA((CHUNKS,)),
            pltpu.SemaphoreType.DMA((7,)),
            pltpu.SemaphoreType.DMA((12,)),
            pltpu.SemaphoreType.DMA((12,)),
        ],
        compiler_params=pltpu.CompilerParams(
            collective_id=0, has_side_effects=True, vmem_limit_bytes=60 * 1024 * 1024
        ),
    )(
        jnp.transpose(section_state, (1, 0, 2)),
        jnp.transpose(base_state, (1, 0, 2)),
        ratio,
        send_list,
        tile_row,
        tile_col,
        tile_flip,
        face_tiles,
    )
    return jnp.transpose(updated, (1, 0, 2))


def solution(mesh):
    return jax.shard_map(
        per_device,
        mesh=mesh,
        in_specs=(
            P(("dom", "sub"), None, None),
            P(("dom", "sub"), None, None),
            P(("dom", "sub"), None),
            P("dom", "sub", None, None),
            P(("dom", "sub"), None, None, None),
            P(("dom", "sub")),
            P(("dom", "sub")),
            P(("dom", "sub")),
        ),
        out_specs=P(("dom", "sub"), None, None),
        check_vma=False,
    )
```

```python
import functools

import jax
import jax.numpy as jnp
from jax import lax
from jax.experimental import pallas as pl
from jax.experimental.pallas import tpu as pltpu
from jax.sharding import PartitionSpec as P

MESH = pl.DeviceIdType.MESH
F32, BF16 = jnp.float32, jnp.bfloat16
CURVE_STEPS = (1, -1, 2, -2)
SUBS = 4
OWN = 8
PART = SUBS * OWN
LIST = 4
TILES = 32
CELLS = 128
SLOTS = PART + len(CURVE_STEPS) * SUBS * LIST
ROWS = 8
CHUNKS = 4
NUM_V = 8
NUM_R = 6


def row_sums(owners, parts):
    x = jnp.concatenate(parts, axis=1)
    high = x.astype(BF16)
    rest = x - high.astype(F32)
    mid = rest.astype(BF16)
    low = (rest - mid.astype(F32)).astype(BF16)
    total = jnp.dot(
        owners, jnp.concatenate([high, mid, low], axis=0), preferred_element_type=F32
    )
    return [total[:, i * CELLS : (i + 1) * CELLS] for i in range(len(parts))]


def kernel(
    doms,
    state_h,
    base_h,
    ratio_h,
    send_h,
    row_h,
    col_h,
    flip_h,
    tiles_h,
    out_ref,
    raw,
    weights,
    absolute,
    state,
    base,
    ratio,
    own,
    packets,
    ext,
    gathered,
    terms,
    part_v,
    recv_v,
    mixed,
    own_v,
    packets_v,
    ext_v,
    gathered_v,
    scaled,
    spread,
    fluxes,
    contribution,
    part_r,
    recv_r,
    send_s,
    row_s,
    col_s,
    flip_s,
    tile_sem,
    load_sem,
    send_sem,
    recv_sem,
):
    me, sub = lax.axis_index("dom"), lax.axis_index("sub")
    peers = [lax.rem(sub + i, SUBS) for i in (2, 1, 3)]
    targets = [me + step for step in CURVE_STEPS]
    inside = lambda dom: (dom >= 0) & (dom < doms)

    barrier = pltpu.get_barrier_semaphore()
    greeted = SUBS - 1
    for target in targets:
        greeted = greeted + jnp.where(inside(target), SUBS, 0)

        @pl.when(inside(target))
        def _():
            for s in range(SUBS):
                pl.semaphore_signal(
                    barrier, inc=1, device_id=(target, jnp.int32(s)), device_id_type=MESH
                )

    for peer in peers:
        pl.semaphore_signal(barrier, inc=1, device_id=(me, peer), device_id_type=MESH)

    loads = [
        pltpu.make_async_copy(state_h, state, load_sem.at[0]),
        pltpu.make_async_copy(base_h, base, load_sem.at[1]),
        pltpu.make_async_copy(ratio_h, ratio, load_sem.at[2]),
        pltpu.make_async_copy(send_h, send_s, load_sem.at[3]),
        pltpu.make_async_copy(row_h, row_s, load_sem.at[4]),
        pltpu.make_async_copy(col_h, col_s, load_sem.at[5]),
        pltpu.make_async_copy(flip_h, flip_s, load_sem.at[6]),
    ]
    for load in loads:
        load.start()
    per_chunk = TILES // CHUNKS
    tile_loads = [
        pltpu.make_async_copy(
            tiles_h.at[pl.ds(c * per_chunk, per_chunk)],
            raw.at[pl.ds(c * per_chunk, per_chunk)],
            tile_sem.at[c],
        )
        for c in range(CHUNKS)
    ]
    for load in tile_loads:
        load.start()

    def remote(source, target, number, device):
        pltpu.make_async_remote_copy(
            src_ref=source,
            dst_ref=target,
            send_sem=send_sem.at[number],
            recv_sem=recv_sem.at[number],
            device_id=device,
            device_id_type=MESH,
        ).start()

    def drain(sems, number, like):
        pltpu.make_async_copy(like, like, sems.at[number]).wait()

    def share(values, lists, extended, rows, first):
        at = sub * OWN
        for k in (2, 3, 1, 0):
            slot = PART + (k * SUBS + sub) * LIST

            @pl.when(inside(targets[k]))
            def _():
                for j in range(LIST):
                    lists[k * LIST + j] = values[jnp.maximum(send_s[0, 0, k, j], 0)]
                for i in (2, 1, 3, 0):
                    remote(
                        lists.at[pl.ds(k * LIST, LIST), pl.ds(0, rows)],
                        extended.at[pl.ds(slot, LIST), pl.ds(0, rows)],
                        first + k,
                        (targets[k], lax.rem(sub + i, SUBS)),
                    )

        for peer in peers:
            remote(
                values.at[:, pl.ds(0, rows)],
                extended.at[pl.ds(at, OWN), pl.ds(0, rows)],
                first + 4,
                (me, peer),
            )
        extended[pl.ds(at, OWN)] = values[...]

    def shared(sems, extended, rows, first, sign):
        for k, step in enumerate(CURVE_STEPS):

            @pl.when(inside(me + sign * step))
            def _():
                drain(sems, first + k, extended.at[pl.ds(0, SUBS * LIST), pl.ds(0, rows)])

        drain(sems, first + 4, extended.at[pl.ds(0, PART - OWN), pl.ds(0, rows)])

    flat = lambda ref: ref.reshape(ref.shape[0] * ROWS, CELLS)

    loads[0].wait()
    loads[3].wait()
    density, energy = state[0], state[4]
    momentum = [state[1 + i] for i in range(3)]
    velocity = [m / density for m in momentum]
    pressure = 0.4 * (
        energy
        - 0.5
        * (momentum[0] * velocity[0] + momentum[1] * velocity[1] + momentum[2] * velocity[2])
    )
    square = velocity[0] * velocity[0] + velocity[1] * velocity[1] + velocity[2] * velocity[2]
    speed = jnp.sqrt(square + 1.4 * pressure / density)
    for i, value in enumerate(
        [density, *velocity, pressure]
    ):
        flat(own)[pl.ds(i, OWN, stride=ROWS), :] = value

    pl.semaphore_wait(barrier, greeted)
    share(own, packets, ext, 5, 0)

    for load in loads[4:]:
        load.wait()
    lane = lax.broadcasted_iota(jnp.int32, (PART, 3 * TILES), 1)
    lane = lax.rem(lane, TILES)
    tile_rows = jnp.zeros((PART, 3 * TILES), jnp.int32)
    for t in range(TILES):
        tile_rows = jnp.where(lane == t, row_s[t], tile_rows)
    block_row = lax.broadcasted_iota(jnp.int32, (PART, 3 * TILES), 0)
    owners = jnp.where(block_row == tile_rows, 1.0, 0.0).astype(BF16)

    def orient(t, carry):
        flipped = jnp.full((CELLS, CELLS), flip_s[t], jnp.int32) == 1
        total = None
        for d in range(3):
            tile = raw[t, d].astype(F32)
            tile = jnp.where(flipped, -tile, tile.T)
            weights[t, :, pl.ds(d * CELLS, CELLS)] = tile.astype(BF16)
            total = jnp.abs(tile) if total is None else total + jnp.abs(tile)
        absolute[t] = total.astype(BF16)
        return carry

    for c in range(CHUNKS):
        tile_loads[c].wait()
        lax.fori_loop(c * per_chunk, (c + 1) * per_chunk, orient, 0)
    ones = jnp.ones((TILES, CELLS), F32)
    scaled[pl.ds(5 * TILES, TILES), :] = ones
    for v in (6, 7):
        scaled[pl.ds(v * TILES, TILES), :] = jnp.zeros_like(ones)
    for d in range(3):
        for v in (5, 6, 7):
            fluxes[pl.ds((d * ROWS + v) * TILES, TILES), :] = jnp.zeros_like(ones)

    shared(recv_sem, ext, 5, 0, -1)

    def slope(u, carry):
        zero = jnp.zeros((ROWS, CELLS), BF16)
        cols = []
        for i in range(2):
            column = ext[col_s[2 * u + i]]
            gathered[pl.ds(pl.multiple_of((2 * u + i) * ROWS, ROWS), ROWS), :] = column
            cols.append(column.astype(BF16))
        left = jnp.concatenate([jnp.concatenate([cols[0], zero], axis=1), jnp.concatenate([zero, cols[1]], axis=1)], axis=0)
        out = jnp.dot(left, jnp.concatenate([weights[2 * u], weights[2 * u + 1]], axis=0), preferred_element_type=F32)
        for i in range(2):
          for d in range(3):
            terms[pl.ds(pl.multiple_of(((2 * u + i) * 3 + d) * ROWS, ROWS), ROWS), :] = out[
                i * ROWS : (i + 1) * ROWS, d * CELLS : (d + 1) * CELLS
            ]
        return carry

    lax.fori_loop(0, TILES // 2, slope, 0, unroll=TILES // 2)

    def term(d, v):
        return terms[pl.ds(d * ROWS + v, TILES, stride=3 * ROWS), :]

    shear = [[term(d, 1 + i) for i in range(3)] for d in range(3)]
    third = (2.0 / 3.0) * (shear[0][0] + shear[1][1] + shear[2][2])
    sums = row_sums(
        owners,
        [
            2.0 * shear[0][0] - third,
            2.0 * shear[1][1] - third,
            shear[0][1] + shear[1][0],
            shear[0][2] + shear[2][0],
            shear[1][2] + shear[2][1],
        ]
        + [term(d, 4) for d in range(3)]
        + [term(d, 0) for d in range(3)],
    )
    rho, v0, v1, v2, press = [flat(ext)[pl.ds(v, PART, stride=ROWS), :] for v in range(5)]
    s00, s11, s01, s02, s12 = [0.3 * s for s in sums[:5]]
    s22 = -(s00 + s11)
    level = press / rho
    heat = [1.46 * (sums[5 + d] - level * sums[8 + d]) / rho for d in range(3)]
    work = [
        s00 * v0 + s01 * v1 + s02 * v2 + heat[0],
        s01 * v0 + s11 * v1 + s12 * v2 + heat[1],
        s02 * v0 + s12 * v1 + s22 * v2 + heat[2],
    ]
    for c, value in enumerate([s00, s11, s01, s02, s12, *work]):
        for s in range(SUBS):
            part_v[pl.ds((s * NUM_V + c) * OWN, OWN), :] = value[s * OWN : (s + 1) * OWN]

    def reduce_to_owners(part, recv, count, number):
        size = count * OWN
        for i, peer in enumerate(peers):
            remote(
                part.at[pl.ds(pl.multiple_of(peer * size, size), size)],
                recv.at[pl.ds(i * size, size)],
                number,
                (me, peer),
            )

    def reduced(part, recv, count, number):
        size = count * OWN
        drain(recv_sem, number, recv)
        total = part[pl.ds(pl.multiple_of(sub * size, size), size), :]
        for i in range(SUBS - 1):
            total = total + recv[pl.ds(i * size, size), :]
        return total

    reduce_to_owners(part_v, recv_v, NUM_V, 10)

    rho, v0, v1, v2, press = [gathered[pl.ds(v, TILES, stride=ROWS), :] for v in range(5)]
    vel = [v0, v1, v2]
    square = v0 * v0 + v1 * v1 + v2 * v2
    ener = 2.5 * press + 0.5 * rho * square
    wave = jnp.sqrt(square + 1.4 * press / rho)
    mom = [rho * v for v in vel]
    for v, value in enumerate([rho, *mom, ener]):
        scaled[pl.ds(v * TILES, TILES), :] = wave * value

    def dissipate(t, carry):
        left = scaled[pl.ds(t, ROWS, stride=TILES), :].astype(BF16)
        spread[pl.ds(pl.multiple_of(t * ROWS, ROWS), ROWS), :] = jnp.dot(
            left, absolute[t], preferred_element_type=F32
        )
        return carry

    lax.fori_loop(0, TILES, dissipate, 0, unroll=TILES)

    mixed[...] = reduced(part_v, recv_v, NUM_V, 10)
    for r in range(OWN):
        own_v[r] = mixed[pl.ds(r, ROWS, stride=OWN), :]
    share(own_v, packets_v, ext_v, ROWS, 5)
    shared(recv_sem, ext_v, ROWS, 5, -1)

    def gather_v(t, carry):
        gathered_v[pl.ds(pl.multiple_of(t * ROWS, ROWS), ROWS), :] = ext_v[col_s[t]]
        return carry

    lax.fori_loop(0, TILES, gather_v, 0, unroll=TILES)
    s00, s11, s01, s02, s12, w0, w1, w2 = [
        gathered_v[pl.ds(c, TILES, stride=ROWS), :] for c in range(NUM_V)
    ]
    stress = [[s00, s01, s02], [s01, s11, s12], [s02, s12, -(s00 + s11)]]
    work = [w0, w1, w2]
    for d in range(3):
        values = [mom[d]]
        for i in range(3):
            flow = mom[i] * vel[d]
            if i == d:
                flow = flow + press
            values.append(flow - stress[d][i])
        values.append((ener + press) * vel[d] - work[d])
        for v, value in enumerate(values):
            fluxes[pl.ds((d * ROWS + v) * TILES, TILES), :] = value

    def flux(t, carry):
        at = pl.multiple_of(t * ROWS, ROWS)
        left = jnp.concatenate(
            [fluxes[pl.ds(d * ROWS * TILES + t, ROWS, stride=TILES), :] for d in range(3)],
            axis=1,
        ).astype(BF16)
        total = jnp.dot(
            left,
            jnp.concatenate([weights[t, :, pl.ds(d * CELLS, CELLS)] for d in range(3)], axis=0),
            preferred_element_type=F32,
        )
        contribution[pl.ds(at, ROWS), :] = total - 0.1 * spread[pl.ds(at, ROWS), :]
        return carry

    lax.fori_loop(0, TILES, flux, 0, unroll=TILES)

    sums = row_sums(
        owners, [contribution[pl.ds(v, TILES, stride=ROWS), :] for v in range(NUM_R)]
    )
    for c, value in enumerate(sums):
        for s in range(SUBS):
            part_r[pl.ds((s * NUM_R + c) * OWN, OWN), :] = value[s * OWN : (s + 1) * OWN]
    reduce_to_owners(part_r, recv_r, NUM_R, 11)

    loads[1].wait()
    loads[2].wait()
    total = reduced(part_r, recv_r, NUM_R, 11)
    absolute_sum = total[5 * OWN : 6 * OWN] * speed
    half = 0.5 * ratio[...]
    for v, value in enumerate([density, *momentum, energy]):
        residual = total[v * OWN : (v + 1) * OWN] - absolute_sum * value
        out_ref[v] = base[v] - half * residual

    shared(send_sem, ext, 5, 0, 1)
    drain(send_sem, 10, recv_v)
    shared(send_sem, ext_v, ROWS, 5, 1)
    drain(send_sem, 11, recv_r)


def per_device(
    section_state, base_state, ratio, send_list, face_tiles, tile_row, tile_col, tile_flip
):
    any_space = pl.BlockSpec(memory_space=pl.ANY)
    scalars = lambda *shape: pltpu.SMEM(shape, jnp.int32)
    blocks = lambda count: pltpu.VMEM((count, ROWS, CELLS), F32)
    row = lambda count: pltpu.VMEM((count, CELLS), F32)
    updated = pl.pallas_call(
        functools.partial(kernel, lax.axis_size("dom")),
        out_shape=jax.ShapeDtypeStruct((5, OWN, CELLS), F32),
        in_specs=[any_space] * 8,
        out_specs=pl.BlockSpec(memory_space=pltpu.VMEM),
        scratch_shapes=[
            pltpu.VMEM((TILES, 3, CELLS, CELLS), BF16),
            pltpu.VMEM((TILES, CELLS, 3 * CELLS), BF16),
            pltpu.VMEM((TILES, CELLS, CELLS), BF16),
            pltpu.VMEM((5, OWN, CELLS), F32),
            pltpu.VMEM((5, OWN, CELLS), F32),
            pltpu.VMEM((OWN, CELLS), F32),
            blocks(OWN),
            blocks(len(CURVE_STEPS) * LIST),
            blocks(SLOTS),
            row(TILES * ROWS),
            row(TILES * 3 * ROWS),
            row(SUBS * NUM_V * OWN),
            row((SUBS - 1) * NUM_V * OWN),
            row(NUM_V * OWN),
            blocks(OWN),
            blocks(len(CURVE_STEPS) * LIST),
            blocks(SLOTS),
            row(TILES * ROWS),
            row(ROWS * TILES),
            row(TILES * ROWS),
            row(3 * ROWS * TILES),
            row(TILES * ROWS),
            row(SUBS * NUM_R * OWN),
            row((SUBS - 1) * NUM_R * OWN),
            scalars(*send_list.shape),
            scalars(TILES),
            scalars(TILES),
            scalars(TILES),
            pltpu.SemaphoreType.DMA((CHUNKS,)),
            pltpu.SemaphoreType.DMA((7,)),
            pltpu.SemaphoreType.DMA((12,)),
            pltpu.SemaphoreType.DMA((12,)),
        ],
        compiler_params=pltpu.CompilerParams(
            collective_id=0, has_side_effects=True, vmem_limit_bytes=60 * 1024 * 1024
        ),
    )(
        jnp.transpose(section_state, (1, 0, 2)),
        jnp.transpose(base_state, (1, 0, 2)),
        ratio,
        send_list,
        tile_row,
        tile_col,
        tile_flip,
        face_tiles,
    )
    return jnp.transpose(updated, (1, 0, 2))


def solution(mesh):
    return jax.shard_map(
        per_device,
        mesh=mesh,
        in_specs=(
            P(("dom", "sub"), None, None),
            P(("dom", "sub"), None, None),
            P(("dom", "sub"), None),
            P("dom", "sub", None, None),
            P(("dom", "sub"), None, None, None),
            P(("dom", "sub")),
            P(("dom", "sub")),
            P(("dom", "sub")),
        ),
        out_specs=P(("dom", "sub"), None, None),
        check_vma=False,
    )
```

```python
import functools

import jax
import jax.numpy as jnp
from jax import lax
from jax.experimental import pallas as pl
from jax.experimental.pallas import tpu as pltpu
from jax.sharding import PartitionSpec as P

MESH = pl.DeviceIdType.MESH
F32, BF16 = jnp.float32, jnp.bfloat16
CURVE_STEPS = (1, -1, 2, -2)
SUBS = 4
OWN = 8
PART = SUBS * OWN
LIST = 4
TILES = 32
CELLS = 128
SLOTS = PART + len(CURVE_STEPS) * SUBS * LIST
ROWS = 8
CHUNKS = 4
NUM_V = 8
NUM_R = 6


def row_sums(owners, parts):
    x = jnp.concatenate(parts, axis=1)
    high = x.astype(BF16)
    rest = x - high.astype(F32)
    mid = rest.astype(BF16)
    low = (rest - mid.astype(F32)).astype(BF16)
    total = jnp.dot(
        owners, jnp.concatenate([high, mid, low], axis=0), preferred_element_type=F32
    )
    return [total[:, i * CELLS : (i + 1) * CELLS] for i in range(len(parts))]


def kernel(
    doms,
    state_h,
    base_h,
    ratio_h,
    send_h,
    row_h,
    col_h,
    flip_h,
    tiles_h,
    out_ref,
    raw,
    weights,
    absolute,
    state,
    base,
    ratio,
    own,
    packets,
    ext,
    gathered,
    terms,
    part_v,
    recv_v,
    mixed,
    own_v,
    packets_v,
    ext_v,
    gathered_v,
    own_w,
    packets_w,
    ext_w,
    gathered_w,
    scaled,
    spread,
    fluxes,
    contribution,
    part_r,
    recv_r,
    send_s,
    row_s,
    col_s,
    flip_s,
    tile_sem,
    load_sem,
    send_sem,
    recv_sem,
):
    me, sub = lax.axis_index("dom"), lax.axis_index("sub")
    peers = [lax.rem(sub + i, SUBS) for i in (2, 1, 3)]
    targets = [me + step for step in CURVE_STEPS]
    inside = lambda dom: (dom >= 0) & (dom < doms)

    barrier = pltpu.get_barrier_semaphore()
    greeted = SUBS - 1
    for target in targets:
        greeted = greeted + jnp.where(inside(target), SUBS, 0)

        @pl.when(inside(target))
        def _():
            for s in range(SUBS):
                pl.semaphore_signal(
                    barrier, inc=1, device_id=(target, jnp.int32(s)), device_id_type=MESH
                )

    for peer in peers:
        pl.semaphore_signal(barrier, inc=1, device_id=(me, peer), device_id_type=MESH)

    loads = [
        pltpu.make_async_copy(state_h, state, load_sem.at[0]),
        pltpu.make_async_copy(base_h, base, load_sem.at[1]),
        pltpu.make_async_copy(ratio_h, ratio, load_sem.at[2]),
        pltpu.make_async_copy(send_h, send_s, load_sem.at[3]),
        pltpu.make_async_copy(row_h, row_s, load_sem.at[4]),
        pltpu.make_async_copy(col_h, col_s, load_sem.at[5]),
        pltpu.make_async_copy(flip_h, flip_s, load_sem.at[6]),
    ]
    for load in loads:
        load.start()
    per_chunk = TILES // CHUNKS
    tile_loads = [
        pltpu.make_async_copy(
            tiles_h.at[pl.ds(c * per_chunk, per_chunk)],
            raw.at[pl.ds(c * per_chunk, per_chunk)],
            tile_sem.at[c],
        )
        for c in range(CHUNKS)
    ]
    for load in tile_loads:
        load.start()

    def remote(source, target, number, device):
        pltpu.make_async_remote_copy(
            src_ref=source,
            dst_ref=target,
            send_sem=send_sem.at[number],
            recv_sem=recv_sem.at[number],
            device_id=device,
            device_id_type=MESH,
        ).start()

    def drain(sems, number, like):
        pltpu.make_async_copy(like, like, sems.at[number]).wait()

    def share(values, lists, extended, rows, first):
        at = sub * OWN
        def pick(k):
            for j in range(LIST):
                lists[k * LIST + j] = values[jnp.maximum(send_s[0, 0, k, j], 0)]

        def send(k, i):
            remote(
                lists.at[pl.ds(k * LIST, LIST), pl.ds(0, rows)],
                extended.at[pl.ds(PART + (k * SUBS + sub) * LIST, LIST), pl.ds(0, rows)],
                first + k,
                (targets[k], lax.rem(sub + i, SUBS)),
            )

        def send_own(which):
            for peer in which:
                remote(
                    values.at[:, pl.ds(0, rows)],
                    extended.at[pl.ds(at, OWN), pl.ds(0, rows)],
                    first + 4,
                    (me, peer),
                )

        for turn in range(2):
            for k in (0, 1):
                @pl.when(inside(targets[k]) & (lax.rem(me + k + turn, 2) == 1))
                def _():
                    pick(k)
                    for i in (2, 1, 3, 0):
                        send(k, i)
            if turn == 0:
                for k in (2, 3):
                    @pl.when(inside(targets[k]))
                    def _():
                        pick(k)
                        for i in (2, 1, 3, 0):
                            send(k, i)
        send_own(peers)
        extended[pl.ds(at, OWN)] = values[...]

    def shared(sems, extended, rows, first, sign):
        for k, step in enumerate(CURVE_STEPS):

            @pl.when(inside(me + sign * step))
            def _():
                drain(sems, first + k, extended.at[pl.ds(0, SUBS * LIST), pl.ds(0, rows)])

        drain(sems, first + 4, extended.at[pl.ds(0, PART - OWN), pl.ds(0, rows)])

    flat = lambda ref: ref.reshape(ref.shape[0] * ROWS, CELLS)

    loads[0].wait()
    loads[3].wait()
    density, energy = state[0], state[4]
    momentum = [state[1 + i] for i in range(3)]
    velocity = [m / density for m in momentum]
    pressure = 0.4 * (
        energy
        - 0.5
        * (momentum[0] * velocity[0] + momentum[1] * velocity[1] + momentum[2] * velocity[2])
    )
    square = velocity[0] * velocity[0] + velocity[1] * velocity[1] + velocity[2] * velocity[2]
    speed = jnp.sqrt(square + 1.4 * pressure / density)
    for i, value in enumerate(
        [density, *velocity, pressure]
    ):
        flat(own)[pl.ds(i, OWN, stride=ROWS), :] = value

    pl.semaphore_wait(barrier, greeted)
    share(own, packets, ext, 5, 0)

    for load in loads[4:]:
        load.wait()
    lane = lax.broadcasted_iota(jnp.int32, (PART, 3 * TILES), 1)
    lane = lax.rem(lane, TILES)
    tile_rows = jnp.zeros((PART, 3 * TILES), jnp.int32)
    for t in range(TILES):
        tile_rows = jnp.where(lane == t, row_s[t], tile_rows)
    block_row = lax.broadcasted_iota(jnp.int32, (PART, 3 * TILES), 0)
    owners = jnp.where(block_row == tile_rows, 1.0, 0.0).astype(BF16)

    def orient(t, carry):
        flipped = jnp.full((CELLS, CELLS), flip_s[t], jnp.int32) == 1
        total = None
        for d in range(3):
            tile = raw[t, d].astype(F32)
            tile = jnp.where(flipped, -tile, tile.T)
            weights[t, :, pl.ds(d * CELLS, CELLS)] = tile.astype(BF16)
            total = jnp.abs(tile) if total is None else total + jnp.abs(tile)
        absolute[t] = total.astype(BF16)
        return carry

    for c in range(CHUNKS):
        tile_loads[c].wait()
        lax.fori_loop(c * per_chunk, (c + 1) * per_chunk, orient, 0)
    ones = jnp.ones((TILES, CELLS), F32)
    scaled[pl.ds(5 * TILES, TILES), :] = ones
    for v in (6, 7):
        scaled[pl.ds(v * TILES, TILES), :] = jnp.zeros_like(ones)
    for d in range(3):
        for v in (5, 6, 7):
            fluxes[pl.ds((d * ROWS + v) * TILES, TILES), :] = jnp.zeros_like(ones)

    shared(recv_sem, ext, 5, 0, -1)

    def slope(u, carry):
        zero = jnp.zeros((ROWS, CELLS), BF16)
        cols = []
        for i in range(2):
            column = ext[col_s[2 * u + i]]
            gathered[pl.ds(pl.multiple_of((2 * u + i) * ROWS, ROWS), ROWS), :] = column
            cols.append(column.astype(BF16))
        left = jnp.concatenate([jnp.concatenate([cols[0], zero], axis=1), jnp.concatenate([zero, cols[1]], axis=1)], axis=0)
        out = jnp.dot(left, jnp.concatenate([weights[2 * u], weights[2 * u + 1]], axis=0), preferred_element_type=F32)
        for i in range(2):
          for d in range(3):
            terms[pl.ds(pl.multiple_of(((2 * u + i) * 3 + d) * ROWS, ROWS), ROWS), :] = out[
                i * ROWS : (i + 1) * ROWS, d * CELLS : (d + 1) * CELLS
            ]
        return carry

    lax.fori_loop(0, TILES // 2, slope, 0, unroll=TILES // 2)

    def term(d, v):
        return terms[pl.ds(d * ROWS + v, TILES, stride=3 * ROWS), :]

    shear = [[term(d, 1 + i) for i in range(3)] for d in range(3)]
    third = (2.0 / 3.0) * (shear[0][0] + shear[1][1] + shear[2][2])
    sums = row_sums(
        owners,
        [
            2.0 * shear[0][0] - third,
            2.0 * shear[1][1] - third,
            shear[0][1] + shear[1][0],
            shear[0][2] + shear[2][0],
            shear[1][2] + shear[2][1],
        ]
        + [term(d, 4) for d in range(3)]
        + [term(d, 0) for d in range(3)],
    )
    rho, v0, v1, v2, press = [flat(ext)[pl.ds(v, PART, stride=ROWS), :] for v in range(5)]
    s00, s11, s01, s02, s12 = [0.3 * s for s in sums[:5]]
    s22 = -(s00 + s11)
    level = press / rho
    heat = [1.46 * (sums[5 + d] - level * sums[8 + d]) / rho for d in range(3)]
    work = [
        s00 * v0 + s01 * v1 + s02 * v2 + heat[0],
        s01 * v0 + s11 * v1 + s12 * v2 + heat[1],
        s02 * v0 + s12 * v1 + s22 * v2 + heat[2],
    ]
    for c, value in enumerate([s00, s01, s02, work[0], s11, s12, work[1], work[2]]):
        for s in range(SUBS):
            part_v[pl.ds((s * NUM_V + c) * OWN, OWN), :] = value[s * OWN : (s + 1) * OWN]

    def reduce_to_owners(part, recv, count, number):
        size = count * OWN
        for i, peer in enumerate(peers):
            remote(
                part.at[pl.ds(pl.multiple_of(peer * size, size), size)],
                recv.at[pl.ds(i * size, size)],
                number,
                (me, peer),
            )

    def reduced(part, recv, count, number):
        size = count * OWN
        drain(recv_sem, number, recv)
        total = part[pl.ds(pl.multiple_of(sub * size, size), size), :]
        for i in range(SUBS - 1):
            total = total + recv[pl.ds(i * size, size), :]
        return total

    size, part_rows = NUM_V * OWN, NUM_V * OWN // 2
    for half in range(2):
        for i, peer in enumerate(peers):
            remote(
                part_v.at[pl.ds(peer * size + half * part_rows, part_rows)],
                recv_v.at[pl.ds(i * size + half * part_rows, part_rows)],
                (10, 17)[half],
                (me, peer),
            )

    rho, v0, v1, v2, press = [gathered[pl.ds(v, TILES, stride=ROWS), :] for v in range(5)]
    vel = [v0, v1, v2]
    square = v0 * v0 + v1 * v1 + v2 * v2
    ener = 2.5 * press + 0.5 * rho * square
    wave = jnp.sqrt(square + 1.4 * press / rho)
    mom = [rho * v for v in vel]
    for v, value in enumerate([rho, *mom, ener]):
        scaled[pl.ds(v * TILES, TILES), :] = wave * value

    def dissipate(t, carry):
        left = scaled[pl.ds(t, ROWS, stride=TILES), :].astype(BF16)
        spread[pl.ds(pl.multiple_of(t * ROWS, ROWS), ROWS), :] = jnp.dot(
            left, absolute[t], preferred_element_type=F32
        )
        return carry

    lax.fori_loop(0, TILES, dissipate, 0, unroll=TILES)

    for half, (mine, listed, extended) in enumerate(
        [(own_v, packets_v, ext_v), (own_w, packets_w, ext_w)]
    ):
        drain(recv_sem, (10, 17)[half], recv_v.at[pl.ds(0, (SUBS - 1) * part_rows)])
        total = part_v[pl.ds(sub * size + half * part_rows, part_rows), :]
        for i in range(SUBS - 1):
            total = total + recv_v[pl.ds(i * size + half * part_rows, part_rows), :]
        mixed[pl.ds(half * part_rows, part_rows), :] = total
        for r in range(OWN):
            mine[r, pl.ds(0, 4), :] = mixed[pl.ds(half * part_rows + r, 4, stride=OWN), :]
        share(mine, listed, extended, 4, 5 + 7 * half)

    def gather_v(t, carry):
        gathered_v[pl.ds(pl.multiple_of(t * ROWS, ROWS), ROWS), :] = ext_v[col_s[t]]
        return carry

    def gather_w(t, carry):
        gathered_w[pl.ds(pl.multiple_of(t * ROWS, ROWS), ROWS), :] = ext_w[col_s[t]]
        return carry

    for d in range(3):
        if d == 0:
            shared(recv_sem, ext_v, 4, 5, -1)
            lax.fori_loop(0, TILES, gather_v, 0, unroll=TILES)
            s00, s01, s02, w0 = [gathered_v[pl.ds(c, TILES, stride=ROWS), :] for c in range(4)]
            stress, work = [[s00, s01, s02]], [w0]
        if d == 1:

            def flux_first(t, carry):
                at = pl.multiple_of(t * ROWS, ROWS)
                left = fluxes[pl.ds(t, ROWS, stride=TILES), :].astype(BF16)
                total = jnp.dot(left, weights[t, :, pl.ds(0, CELLS)], preferred_element_type=F32)
                contribution[pl.ds(at, ROWS), :] = total - 0.1 * spread[pl.ds(at, ROWS), :]
                return carry

            lax.fori_loop(0, TILES, flux_first, 0, unroll=TILES)
            shared(recv_sem, ext_w, 4, 12, -1)
            lax.fori_loop(0, TILES, gather_w, 0, unroll=TILES)
            s11, s12, w1, w2 = [gathered_w[pl.ds(c, TILES, stride=ROWS), :] for c in range(4)]
            stress += [[s01, s11, s12], [s02, s12, -(s00 + s11)]]
            work += [w1, w2]
        values = [mom[d]]
        for i in range(3):
            flow = mom[i] * vel[d]
            if i == d:
                flow = flow + press
            values.append(flow - stress[d][i])
        values.append((ener + press) * vel[d] - work[d])
        for v, value in enumerate(values):
            fluxes[pl.ds((d * ROWS + v) * TILES, TILES), :] = value

    def flux(t, carry):
        at = pl.multiple_of(t * ROWS, ROWS)
        left = jnp.concatenate(
            [fluxes[pl.ds(d * ROWS * TILES + t, ROWS, stride=TILES), :] for d in (1, 2)],
            axis=1,
        ).astype(BF16)
        total = jnp.dot(
            left,
            jnp.concatenate([weights[t, :, pl.ds(d * CELLS, CELLS)] for d in (1, 2)], axis=0),
            preferred_element_type=F32,
        )
        contribution[pl.ds(at, ROWS), :] += total
        return carry

    lax.fori_loop(0, TILES, flux, 0, unroll=TILES)

    sums = row_sums(
        owners, [contribution[pl.ds(v, TILES, stride=ROWS), :] for v in range(NUM_R)]
    )
    for c, value in enumerate(sums):
        for s in range(SUBS):
            part_r[pl.ds((s * NUM_R + c) * OWN, OWN), :] = value[s * OWN : (s + 1) * OWN]
    reduce_to_owners(part_r, recv_r, NUM_R, 11)

    loads[1].wait()
    loads[2].wait()
    total = reduced(part_r, recv_r, NUM_R, 11)
    absolute_sum = total[5 * OWN : 6 * OWN] * speed
    half = 0.5 * ratio[...]
    for v, value in enumerate([density, *momentum, energy]):
        residual = total[v * OWN : (v + 1) * OWN] - absolute_sum * value
        out_ref[v] = base[v] - half * residual

    shared(send_sem, ext, 5, 0, 1)
    for number in (10, 17):
        drain(send_sem, number, recv_v.at[pl.ds(0, (SUBS - 1) * part_rows)])
    shared(send_sem, ext_v, 4, 5, 1)
    shared(send_sem, ext_w, 4, 12, 1)
    drain(send_sem, 11, recv_r)


def per_device(
    section_state, base_state, ratio, send_list, face_tiles, tile_row, tile_col, tile_flip
):
    any_space = pl.BlockSpec(memory_space=pl.ANY)
    scalars = lambda *shape: pltpu.SMEM(shape, jnp.int32)
    blocks = lambda count: pltpu.VMEM((count, ROWS, CELLS), F32)
    row = lambda count: pltpu.VMEM((count, CELLS), F32)
    updated = pl.pallas_call(
        functools.partial(kernel, lax.axis_size("dom")),
        out_shape=jax.ShapeDtypeStruct((5, OWN, CELLS), F32),
        in_specs=[any_space] * 8,
        out_specs=pl.BlockSpec(memory_space=pltpu.VMEM),
        scratch_shapes=[
            pltpu.VMEM((TILES, 3, CELLS, CELLS), BF16),
            pltpu.VMEM((TILES, CELLS, 3 * CELLS), BF16),
            pltpu.VMEM((TILES, CELLS, CELLS), BF16),
            pltpu.VMEM((5, OWN, CELLS), F32),
            pltpu.VMEM((5, OWN, CELLS), F32),
            pltpu.VMEM((OWN, CELLS), F32),
            blocks(OWN),
            blocks(len(CURVE_STEPS) * LIST),
            blocks(SLOTS),
            row(TILES * ROWS),
            row(TILES * 3 * ROWS),
            row(SUBS * NUM_V * OWN),
            row((SUBS - 1) * NUM_V * OWN),
            row(NUM_V * OWN),
            blocks(OWN),
            blocks(len(CURVE_STEPS) * LIST),
            blocks(SLOTS),
            row(TILES * ROWS),
            blocks(OWN),
            blocks(len(CURVE_STEPS) * LIST),
            blocks(SLOTS),
            row(TILES * ROWS),
            row(ROWS * TILES),
            row(TILES * ROWS),
            row(3 * ROWS * TILES),
            row(TILES * ROWS),
            row(SUBS * NUM_R * OWN),
            row((SUBS - 1) * NUM_R * OWN),
            scalars(*send_list.shape),
            scalars(TILES),
            scalars(TILES),
            scalars(TILES),
            pltpu.SemaphoreType.DMA((CHUNKS,)),
            pltpu.SemaphoreType.DMA((7,)),
            pltpu.SemaphoreType.DMA((18,)),
            pltpu.SemaphoreType.DMA((18,)),
        ],
        compiler_params=pltpu.CompilerParams(
            collective_id=0, has_side_effects=True, vmem_limit_bytes=60 * 1024 * 1024
        ),
    )(
        jnp.transpose(section_state, (1, 0, 2)),
        jnp.transpose(base_state, (1, 0, 2)),
        ratio,
        send_list,
        tile_row,
        tile_col,
        tile_flip,
        face_tiles,
    )
    return jnp.transpose(updated, (1, 0, 2))


def solution(mesh):
    return jax.shard_map(
        per_device,
        mesh=mesh,
        in_specs=(
            P(("dom", "sub"), None, None),
            P(("dom", "sub"), None, None),
            P(("dom", "sub"), None),
            P("dom", "sub", None, None),
            P(("dom", "sub"), None, None, None),
            P(("dom", "sub")),
            P(("dom", "sub")),
            P(("dom", "sub")),
        ),
        out_specs=P(("dom", "sub"), None, None),
        check_vma=False,
    )
```

```python
import functools

import jax
import jax.numpy as jnp
from jax import lax
from jax.experimental import pallas as pl
from jax.experimental.pallas import tpu as pltpu
from jax.sharding import PartitionSpec as P

MESH = pl.DeviceIdType.MESH
F32, BF16 = jnp.float32, jnp.bfloat16
CURVE_STEPS = (1, -1, 2, -2)
SUBS = 4
OWN = 8
PART = SUBS * OWN
LIST = 4
TILES = 32
CELLS = 128
SLOTS = PART + len(CURVE_STEPS) * SUBS * LIST
ROWS = 8
CHUNKS = 4
NUM_V = 8
NUM_R = 6


def row_sums(owners, parts):
    x = jnp.concatenate(parts, axis=1)
    high = x.astype(BF16)
    rest = x - high.astype(F32)
    mid = rest.astype(BF16)
    low = (rest - mid.astype(F32)).astype(BF16)
    total = jnp.dot(
        owners, jnp.concatenate([high, mid, low], axis=0), preferred_element_type=F32
    )
    return [total[:, i * CELLS : (i + 1) * CELLS] for i in range(len(parts))]


def kernel(
    doms,
    state_h,
    base_h,
    ratio_h,
    send_h,
    row_h,
    col_h,
    flip_h,
    tiles_h,
    out_ref,
    raw,
    weights,
    absolute,
    state,
    base,
    ratio,
    own,
    packets,
    ext,
    gathered,
    terms,
    part_v,
    recv_v,
    mixed,
    own_v,
    packets_v,
    ext_v,
    gathered_v,
    own_w,
    packets_w,
    ext_w,
    gathered_w,
    scaled,
    spread,
    fluxes,
    contribution,
    part_r,
    recv_r,
    send_s,
    row_s,
    col_s,
    flip_s,
    tile_sem,
    load_sem,
    send_sem,
    recv_sem,
):
    me, sub = lax.axis_index("dom"), lax.axis_index("sub")
    peers = [lax.rem(sub + i, SUBS) for i in (2, 1, 3)]
    targets = [me + step for step in CURVE_STEPS]
    inside = lambda dom: (dom >= 0) & (dom < doms)

    barrier = pltpu.get_barrier_semaphore()
    greeted = SUBS - 1
    for target in targets:
        greeted = greeted + jnp.where(inside(target), SUBS, 0)

        @pl.when(inside(target))
        def _():
            for s in range(SUBS):
                pl.semaphore_signal(
                    barrier, inc=1, device_id=(target, jnp.int32(s)), device_id_type=MESH
                )

    for peer in peers:
        pl.semaphore_signal(barrier, inc=1, device_id=(me, peer), device_id_type=MESH)

    loads = [
        pltpu.make_async_copy(state_h, state, load_sem.at[0]),
        pltpu.make_async_copy(base_h, base, load_sem.at[1]),
        pltpu.make_async_copy(ratio_h, ratio, load_sem.at[2]),
        pltpu.make_async_copy(send_h, send_s, load_sem.at[3]),
        pltpu.make_async_copy(row_h, row_s, load_sem.at[4]),
        pltpu.make_async_copy(col_h, col_s, load_sem.at[5]),
        pltpu.make_async_copy(flip_h, flip_s, load_sem.at[6]),
    ]
    for load in loads:
        load.start()
    per_chunk = TILES // CHUNKS
    tile_loads = [
        pltpu.make_async_copy(
            tiles_h.at[pl.ds(c * per_chunk, per_chunk)],
            raw.at[pl.ds(c * per_chunk, per_chunk)],
            tile_sem.at[c],
        )
        for c in range(CHUNKS)
    ]
    for load in tile_loads:
        load.start()

    def remote(source, target, number, device):
        pltpu.make_async_remote_copy(
            src_ref=source,
            dst_ref=target,
            send_sem=send_sem.at[number],
            recv_sem=recv_sem.at[number],
            device_id=device,
            device_id_type=MESH,
        ).start()

    def drain(sems, number, like):
        pltpu.make_async_copy(like, like, sems.at[number]).wait()

    def share(values, lists, extended, rows, first, order):
        def send(k):
            for j in range(LIST):
                lists[k * LIST + j] = values[jnp.maximum(send_s[0, 0, k, j], 0)]
            for i in (2, 1, 3, 0):
                remote(
                    lists.at[pl.ds(k * LIST, LIST), pl.ds(0, rows)],
                    extended.at[pl.ds(PART + (k * SUBS + sub) * LIST, LIST), pl.ds(0, rows)],
                    first + k,
                    (targets[k], lax.rem(sub + i, SUBS)),
                )

        core = lax.rem(me, 2)
        for k in order:
            other_chip = True if k > 1 else core != k
            pl.when(inside(targets[k]) & other_chip)(functools.partial(send, k))
        for k in (0, 1):
            pl.when(inside(targets[k]) & (core == k))(functools.partial(send, k))
        for peer in peers:
            remote(
                values.at[:, pl.ds(0, rows)],
                extended.at[pl.ds(sub * OWN, OWN), pl.ds(0, rows)],
                first + 4,
                (me, peer),
            )
        extended[pl.ds(sub * OWN, OWN)] = values[...]

    def shared(sems, extended, rows, first, sign):
        for k, step in enumerate(CURVE_STEPS):

            @pl.when(inside(me + sign * step))
            def _():
                drain(sems, first + k, extended.at[pl.ds(0, SUBS * LIST), pl.ds(0, rows)])

        drain(sems, first + 4, extended.at[pl.ds(0, PART - OWN), pl.ds(0, rows)])

    flat = lambda ref: ref.reshape(ref.shape[0] * ROWS, CELLS)

    loads[0].wait()
    loads[3].wait()
    density, energy = state[0], state[4]
    momentum = [state[1 + i] for i in range(3)]
    velocity = [m / density for m in momentum]
    pressure = 0.4 * (
        energy
        - 0.5
        * (momentum[0] * velocity[0] + momentum[1] * velocity[1] + momentum[2] * velocity[2])
    )
    square = velocity[0] * velocity[0] + velocity[1] * velocity[1] + velocity[2] * velocity[2]
    speed = jnp.sqrt(square + 1.4 * pressure / density)
    for i, value in enumerate(
        [density, *velocity, pressure]
    ):
        flat(own)[pl.ds(i, OWN, stride=ROWS), :] = value

    pl.semaphore_wait(barrier, greeted)
    share(own, packets, ext, 5, 0, (3, 1, 0, 2))

    for load in loads[4:]:
        load.wait()
    lane = lax.broadcasted_iota(jnp.int32, (PART, 3 * TILES), 1)
    lane = lax.rem(lane, TILES)
    tile_rows = jnp.zeros((PART, 3 * TILES), jnp.int32)
    for t in range(TILES):
        tile_rows = jnp.where(lane == t, row_s[t], tile_rows)
    block_row = lax.broadcasted_iota(jnp.int32, (PART, 3 * TILES), 0)
    owners = jnp.where(block_row == tile_rows, 1.0, 0.0).astype(BF16)

    def orient(t, carry):
        flipped = jnp.full((CELLS, CELLS), flip_s[t], jnp.int32) == 1
        total = None
        for d in range(3):
            tile = raw[t, d].astype(F32)
            tile = jnp.where(flipped, -tile, tile.T)
            weights[t, :, pl.ds(d * CELLS, CELLS)] = tile.astype(BF16)
            total = jnp.abs(tile) if total is None else total + jnp.abs(tile)
        absolute[t] = total.astype(BF16)
        return carry

    for c in range(CHUNKS):
        tile_loads[c].wait()
        lax.fori_loop(c * per_chunk, (c + 1) * per_chunk, orient, 0)
    ones = jnp.ones((TILES, CELLS), F32)
    scaled[pl.ds(5 * TILES, TILES), :] = ones
    for v in (6, 7):
        scaled[pl.ds(v * TILES, TILES), :] = jnp.zeros_like(ones)
    for d in range(3):
        for v in (5, 6, 7):
            fluxes[pl.ds((d * ROWS + v) * TILES, TILES), :] = jnp.zeros_like(ones)

    shared(recv_sem, ext, 5, 0, -1)

    def slope(u, carry):
        zero = jnp.zeros((ROWS, CELLS), BF16)
        cols = []
        for i in range(2):
            column = ext[col_s[2 * u + i]]
            gathered[pl.ds(pl.multiple_of((2 * u + i) * ROWS, ROWS), ROWS), :] = column
            cols.append(column.astype(BF16))
        left = jnp.concatenate([jnp.concatenate([cols[0], zero], axis=1), jnp.concatenate([zero, cols[1]], axis=1)], axis=0)
        out = jnp.dot(left, jnp.concatenate([weights[2 * u], weights[2 * u + 1]], axis=0), preferred_element_type=F32)
        for i in range(2):
          for d in range(3):
            terms[pl.ds(pl.multiple_of(((2 * u + i) * 3 + d) * ROWS, ROWS), ROWS), :] = out[
                i * ROWS : (i + 1) * ROWS, d * CELLS : (d + 1) * CELLS
            ]
        return carry

    lax.fori_loop(0, TILES // 2, slope, 0, unroll=TILES // 2)

    def term(d, v):
        return terms[pl.ds(d * ROWS + v, TILES, stride=3 * ROWS), :]

    shear = [[term(d, 1 + i) for i in range(3)] for d in range(3)]
    third = (2.0 / 3.0) * (shear[0][0] + shear[1][1] + shear[2][2])
    sums = row_sums(
        owners,
        [
            2.0 * shear[0][0] - third,
            2.0 * shear[1][1] - third,
            shear[0][1] + shear[1][0],
            shear[0][2] + shear[2][0],
            shear[1][2] + shear[2][1],
        ]
        + [term(d, 4) for d in range(3)]
        + [term(d, 0) for d in range(3)],
    )
    rho, v0, v1, v2, press = [flat(ext)[pl.ds(v, PART, stride=ROWS), :] for v in range(5)]
    s00, s11, s01, s02, s12 = [0.3 * s for s in sums[:5]]
    s22 = -(s00 + s11)
    level = press / rho
    heat = [1.46 * (sums[5 + d] - level * sums[8 + d]) / rho for d in range(3)]
    work = [
        s00 * v0 + s01 * v1 + s02 * v2 + heat[0],
        s01 * v0 + s11 * v1 + s12 * v2 + heat[1],
        s02 * v0 + s12 * v1 + s22 * v2 + heat[2],
    ]
    for c, value in enumerate([s00, s01, s02, work[0], s11, s12, work[1], work[2]]):
        for s in range(SUBS):
            part_v[pl.ds((s * NUM_V + c) * OWN, OWN), :] = value[s * OWN : (s + 1) * OWN]

    def reduce_to_owners(part, recv, count, number):
        size = count * OWN
        for i, peer in enumerate(peers):
            remote(
                part.at[pl.ds(pl.multiple_of(peer * size, size), size)],
                recv.at[pl.ds(i * size, size)],
                number,
                (me, peer),
            )

    def reduced(part, recv, count, number):
        size = count * OWN
        drain(recv_sem, number, recv)
        total = part[pl.ds(pl.multiple_of(sub * size, size), size), :]
        for i in range(SUBS - 1):
            total = total + recv[pl.ds(i * size, size), :]
        return total

    size, part_rows = NUM_V * OWN, NUM_V * OWN // 2
    for half in range(2):
        for i, peer in enumerate(peers):
            remote(
                part_v.at[pl.ds(peer * size + half * part_rows, part_rows)],
                recv_v.at[pl.ds(i * size + half * part_rows, part_rows)],
                (10, 17)[half],
                (me, peer),
            )

    rho, v0, v1, v2, press = [gathered[pl.ds(v, TILES, stride=ROWS), :] for v in range(5)]
    vel = [v0, v1, v2]
    square = v0 * v0 + v1 * v1 + v2 * v2
    ener = 2.5 * press + 0.5 * rho * square
    wave = jnp.sqrt(square + 1.4 * press / rho)
    mom = [rho * v for v in vel]
    for v, value in enumerate([rho, *mom, ener]):
        scaled[pl.ds(v * TILES, TILES), :] = wave * value

    def dissipate(t, carry):
        left = scaled[pl.ds(t, ROWS, stride=TILES), :].astype(BF16)
        spread[pl.ds(pl.multiple_of(t * ROWS, ROWS), ROWS), :] = jnp.dot(
            left, absolute[t], preferred_element_type=F32
        )
        return carry

    lax.fori_loop(0, TILES, dissipate, 0, unroll=TILES)

    for half, (mine, listed, extended) in enumerate(
        [(own_v, packets_v, ext_v), (own_w, packets_w, ext_w)]
    ):
        drain(recv_sem, (10, 17)[half], recv_v.at[pl.ds(0, (SUBS - 1) * part_rows)])
        total = part_v[pl.ds(sub * size + half * part_rows, part_rows), :]
        for i in range(SUBS - 1):
            total = total + recv_v[pl.ds(i * size + half * part_rows, part_rows), :]
        mixed[pl.ds(half * part_rows, part_rows), :] = total
        for r in range(OWN):
            mine[r, pl.ds(0, 4), :] = mixed[pl.ds(half * part_rows + r, 4, stride=OWN), :]
        share(mine, listed, extended, 4, 5 + 7 * half, (2, 0, 1, 3))

    def gather_v(t, carry):
        gathered_v[pl.ds(pl.multiple_of(t * ROWS, ROWS), ROWS), :] = ext_v[col_s[t]]
        return carry

    def gather_w(t, carry):
        gathered_w[pl.ds(pl.multiple_of(t * ROWS, ROWS), ROWS), :] = ext_w[col_s[t]]
        return carry

    for d in range(3):
        if d == 0:
            shared(recv_sem, ext_v, 4, 5, -1)
            lax.fori_loop(0, TILES, gather_v, 0, unroll=TILES)
            s00, s01, s02, w0 = [gathered_v[pl.ds(c, TILES, stride=ROWS), :] for c in range(4)]
            stress, work = [[s00, s01, s02]], [w0]
        if d == 1:

            def flux_first(t, carry):
                at = pl.multiple_of(t * ROWS, ROWS)
                left = fluxes[pl.ds(t, ROWS, stride=TILES), :].astype(BF16)
                total = jnp.dot(left, weights[t, :, pl.ds(0, CELLS)], preferred_element_type=F32)
                contribution[pl.ds(at, ROWS), :] = total - 0.1 * spread[pl.ds(at, ROWS), :]
                return carry

            lax.fori_loop(0, TILES, flux_first, 0, unroll=TILES)
            shared(recv_sem, ext_w, 4, 12, -1)
            lax.fori_loop(0, TILES, gather_w, 0, unroll=TILES)
            s11, s12, w1, w2 = [gathered_w[pl.ds(c, TILES, stride=ROWS), :] for c in range(4)]
            stress += [[s01, s11, s12], [s02, s12, -(s00 + s11)]]
            work += [w1, w2]
        values = [mom[d]]
        for i in range(3):
            flow = mom[i] * vel[d]
            if i == d:
                flow = flow + press
            values.append(flow - stress[d][i])
        values.append((ener + press) * vel[d] - work[d])
        for v, value in enumerate(values):
            fluxes[pl.ds((d * ROWS + v) * TILES, TILES), :] = value

    def flux(t, carry):
        at = pl.multiple_of(t * ROWS, ROWS)
        left = jnp.concatenate(
            [fluxes[pl.ds(d * ROWS * TILES + t, ROWS, stride=TILES), :] for d in (1, 2)],
            axis=1,
        ).astype(BF16)
        total = jnp.dot(
            left,
            jnp.concatenate([weights[t, :, pl.ds(d * CELLS, CELLS)] for d in (1, 2)], axis=0),
            preferred_element_type=F32,
        )
        contribution[pl.ds(at, ROWS), :] += total
        return carry

    lax.fori_loop(0, TILES, flux, 0, unroll=TILES)

    sums = row_sums(
        owners, [contribution[pl.ds(v, TILES, stride=ROWS), :] for v in range(NUM_R)]
    )
    for c, value in enumerate(sums):
        for s in range(SUBS):
            part_r[pl.ds((s * NUM_R + c) * OWN, OWN), :] = value[s * OWN : (s + 1) * OWN]
    reduce_to_owners(part_r, recv_r, NUM_R, 11)

    loads[1].wait()
    loads[2].wait()
    total = reduced(part_r, recv_r, NUM_R, 11)
    absolute_sum = total[5 * OWN : 6 * OWN] * speed
    half = 0.5 * ratio[...]
    for v, value in enumerate([density, *momentum, energy]):
        residual = total[v * OWN : (v + 1) * OWN] - absolute_sum * value
        out_ref[v] = base[v] - half * residual

    shared(send_sem, ext, 5, 0, 1)
    for number in (10, 17):
        drain(send_sem, number, recv_v.at[pl.ds(0, (SUBS - 1) * part_rows)])
    shared(send_sem, ext_v, 4, 5, 1)
    shared(send_sem, ext_w, 4, 12, 1)
    drain(send_sem, 11, recv_r)


def per_device(
    section_state, base_state, ratio, send_list, face_tiles, tile_row, tile_col, tile_flip
):
    any_space = pl.BlockSpec(memory_space=pl.ANY)
    scalars = lambda *shape: pltpu.SMEM(shape, jnp.int32)
    blocks = lambda count: pltpu.VMEM((count, ROWS, CELLS), F32)
    row = lambda count: pltpu.VMEM((count, CELLS), F32)
    updated = pl.pallas_call(
        functools.partial(kernel, lax.axis_size("dom")),
        out_shape=jax.ShapeDtypeStruct((5, OWN, CELLS), F32),
        in_specs=[any_space] * 8,
        out_specs=pl.BlockSpec(memory_space=pltpu.VMEM),
        scratch_shapes=[
            pltpu.VMEM((TILES, 3, CELLS, CELLS), BF16),
            pltpu.VMEM((TILES, CELLS, 3 * CELLS), BF16),
            pltpu.VMEM((TILES, CELLS, CELLS), BF16),
            pltpu.VMEM((5, OWN, CELLS), F32),
            pltpu.VMEM((5, OWN, CELLS), F32),
            pltpu.VMEM((OWN, CELLS), F32),
            blocks(OWN),
            blocks(len(CURVE_STEPS) * LIST),
            blocks(SLOTS),
            row(TILES * ROWS),
            row(TILES * 3 * ROWS),
            row(SUBS * NUM_V * OWN),
            row((SUBS - 1) * NUM_V * OWN),
            row(NUM_V * OWN),
            blocks(OWN),
            blocks(len(CURVE_STEPS) * LIST),
            blocks(SLOTS),
            row(TILES * ROWS),
            blocks(OWN),
            blocks(len(CURVE_STEPS) * LIST),
            blocks(SLOTS),
            row(TILES * ROWS),
            row(ROWS * TILES),
            row(TILES * ROWS),
            row(3 * ROWS * TILES),
            row(TILES * ROWS),
            row(SUBS * NUM_R * OWN),
            row((SUBS - 1) * NUM_R * OWN),
            scalars(*send_list.shape),
            scalars(TILES),
            scalars(TILES),
            scalars(TILES),
            pltpu.SemaphoreType.DMA((CHUNKS,)),
            pltpu.SemaphoreType.DMA((7,)),
            pltpu.SemaphoreType.DMA((18,)),
            pltpu.SemaphoreType.DMA((18,)),
        ],
        compiler_params=pltpu.CompilerParams(
            collective_id=0, has_side_effects=True, vmem_limit_bytes=60 * 1024 * 1024
        ),
    )(
        jnp.transpose(section_state, (1, 0, 2)),
        jnp.transpose(base_state, (1, 0, 2)),
        ratio,
        send_list,
        tile_row,
        tile_col,
        tile_flip,
        face_tiles,
    )
    return jnp.transpose(updated, (1, 0, 2))


def solution(mesh):
    return jax.shard_map(
        per_device,
        mesh=mesh,
        in_specs=(
            P(("dom", "sub"), None, None),
            P(("dom", "sub"), None, None),
            P(("dom", "sub"), None),
            P("dom", "sub", None, None),
            P(("dom", "sub"), None, None, None),
            P(("dom", "sub")),
            P(("dom", "sub")),
            P(("dom", "sub")),
        ),
        out_specs=P(("dom", "sub"), None, None),
        check_vma=False,
    )
```

```python
import functools

import jax
import jax.numpy as jnp
from jax import lax
from jax.experimental import pallas as pl
from jax.experimental.pallas import tpu as pltpu
from jax.sharding import PartitionSpec as P

MESH = pl.DeviceIdType.MESH
F32, BF16 = jnp.float32, jnp.bfloat16
CURVE_STEPS = (1, -1, 2, -2)
SUBS = 4
OWN = 8
PART = SUBS * OWN
LIST = 4
TILES = 32
CELLS = 128
SLOTS = PART + len(CURVE_STEPS) * SUBS * LIST
ROWS = 8
CHUNKS = 4
NUM_V = 8
NUM_R = 6


def row_sums(owners, parts):
    x = jnp.concatenate(parts, axis=1)
    high = x.astype(BF16)
    rest = x - high.astype(F32)
    mid = rest.astype(BF16)
    low = (rest - mid.astype(F32)).astype(BF16)
    total = jnp.dot(
        owners, jnp.concatenate([high, mid, low], axis=0), preferred_element_type=F32
    )
    return [total[:, i * CELLS : (i + 1) * CELLS] for i in range(len(parts))]


def kernel(
    doms,
    state_h,
    base_h,
    ratio_h,
    send_h,
    row_h,
    col_h,
    flip_h,
    tiles_h,
    out_ref,
    raw,
    weights,
    absolute,
    state,
    base,
    ratio,
    own,
    packets,
    ext,
    gathered,
    terms,
    part_v,
    recv_v,
    mixed,
    own_v,
    packets_v,
    ext_v,
    gathered_v,
    own_w,
    packets_w,
    ext_w,
    gathered_w,
    scaled,
    spread,
    fluxes,
    contribution,
    part_r,
    recv_r,
    send_s,
    row_s,
    col_s,
    flip_s,
    tile_sem,
    load_sem,
    send_sem,
    recv_sem,
):
    me, sub = lax.axis_index("dom"), lax.axis_index("sub")
    peers = [lax.rem(sub + i, SUBS) for i in (2, 1, 3)]
    targets = [me + step for step in CURVE_STEPS]
    inside = lambda dom: (dom >= 0) & (dom < doms)

    barrier = pltpu.get_barrier_semaphore()
    greeted = SUBS - 1
    for target in targets:
        greeted = greeted + jnp.where(inside(target), SUBS, 0)

        @pl.when(inside(target))
        def _():
            for s in range(SUBS):
                pl.semaphore_signal(
                    barrier, inc=1, device_id=(target, jnp.int32(s)), device_id_type=MESH
                )

    for peer in peers:
        pl.semaphore_signal(barrier, inc=1, device_id=(me, peer), device_id_type=MESH)

    loads = [
        pltpu.make_async_copy(state_h, state, load_sem.at[0]),
        pltpu.make_async_copy(base_h, base, load_sem.at[1]),
        pltpu.make_async_copy(ratio_h, ratio, load_sem.at[2]),
        pltpu.make_async_copy(send_h, send_s, load_sem.at[3]),
        pltpu.make_async_copy(row_h, row_s, load_sem.at[4]),
        pltpu.make_async_copy(col_h, col_s, load_sem.at[5]),
        pltpu.make_async_copy(flip_h, flip_s, load_sem.at[6]),
    ]
    for load in loads:
        load.start()
    per_chunk = TILES // CHUNKS
    tile_loads = [
        pltpu.make_async_copy(
            tiles_h.at[pl.ds(c * per_chunk, per_chunk)],
            raw.at[pl.ds(c * per_chunk, per_chunk)],
            tile_sem.at[c],
        )
        for c in range(CHUNKS)
    ]
    for load in tile_loads:
        load.start()

    def remote(source, target, number, device):
        pltpu.make_async_remote_copy(
            src_ref=source,
            dst_ref=target,
            send_sem=send_sem.at[number],
            recv_sem=recv_sem.at[number],
            device_id=device,
            device_id_type=MESH,
        ).start()

    def drain(sems, number, like):
        pltpu.make_async_copy(like, like, sems.at[number]).wait()

    core = lax.rem(me, 2)

    def share_lists(values, lists, extended, rows, first, order):
        def send(k):
            for j in range(LIST):
                lists[k * LIST + j] = values[jnp.maximum(send_s[0, 0, k, j], 0)]
            for i in (2, 1, 3, 0):
                remote(
                    lists.at[pl.ds(k * LIST, LIST), pl.ds(0, rows)],
                    extended.at[pl.ds(PART + (k * SUBS + sub) * LIST, LIST), pl.ds(0, rows)],
                    first + k,
                    (targets[k], lax.rem(sub + i, SUBS)),
                )

        for k, where in order:
            pl.when(inside(targets[k]) & where)(functools.partial(send, k))

    def share_own(values, extended, rows, first):
        for peer in peers:
            remote(
                values.at[:, pl.ds(0, rows)],
                extended.at[pl.ds(sub * OWN, OWN), pl.ds(0, rows)],
                first + 4,
                (me, peer),
            )
        extended[pl.ds(sub * OWN, OWN)] = values[...]

    later = [(2, True), (0, core == 1)]
    earlier = [(3, True), (1, core == 0)]
    same_chip = [(0, core == 0), (1, core == 1)]

    def shared(sems, extended, rows, first, sign):
        for k, step in enumerate(CURVE_STEPS):

            @pl.when(inside(me + sign * step))
            def _():
                drain(sems, first + k, extended.at[pl.ds(0, SUBS * LIST), pl.ds(0, rows)])

        drain(sems, first + 4, extended.at[pl.ds(0, PART - OWN), pl.ds(0, rows)])

    flat = lambda ref: ref.reshape(ref.shape[0] * ROWS, CELLS)

    loads[0].wait()
    loads[3].wait()
    density, energy = state[0], state[4]
    momentum = [state[1 + i] for i in range(3)]
    velocity = [m / density for m in momentum]
    pressure = 0.4 * (
        energy
        - 0.5
        * (momentum[0] * velocity[0] + momentum[1] * velocity[1] + momentum[2] * velocity[2])
    )
    square = velocity[0] * velocity[0] + velocity[1] * velocity[1] + velocity[2] * velocity[2]
    speed = jnp.sqrt(square + 1.4 * pressure / density)
    for i, value in enumerate(
        [density, *velocity, pressure]
    ):
        flat(own)[pl.ds(i, OWN, stride=ROWS), :] = value

    pl.semaphore_wait(barrier, greeted)
    share_lists(own, packets, ext, 5, 0, earlier + later + same_chip)
    share_own(own, ext, 5, 0)

    for load in loads[4:]:
        load.wait()
    lane = lax.broadcasted_iota(jnp.int32, (PART, 3 * TILES), 1)
    lane = lax.rem(lane, TILES)
    tile_rows = jnp.zeros((PART, 3 * TILES), jnp.int32)
    for t in range(TILES):
        tile_rows = jnp.where(lane == t, row_s[t], tile_rows)
    block_row = lax.broadcasted_iota(jnp.int32, (PART, 3 * TILES), 0)
    owners = jnp.where(block_row == tile_rows, 1.0, 0.0).astype(BF16)

    def orient(t, carry):
        flipped = jnp.full((CELLS, CELLS), flip_s[t], jnp.int32) == 1
        total = None
        for d in range(3):
            tile = raw[t, d].astype(F32)
            tile = jnp.where(flipped, -tile, tile.T)
            weights[t, :, pl.ds(d * CELLS, CELLS)] = tile.astype(BF16)
            total = jnp.abs(tile) if total is None else total + jnp.abs(tile)
        absolute[t] = total.astype(BF16)
        return carry

    for c in range(CHUNKS):
        tile_loads[c].wait()
        lax.fori_loop(c * per_chunk, (c + 1) * per_chunk, orient, 0)
    ones = jnp.ones((TILES, CELLS), F32)
    scaled[pl.ds(5 * TILES, TILES), :] = ones
    for v in (6, 7):
        scaled[pl.ds(v * TILES, TILES), :] = jnp.zeros_like(ones)
    for d in range(3):
        for v in (5, 6, 7):
            fluxes[pl.ds((d * ROWS + v) * TILES, TILES), :] = jnp.zeros_like(ones)

    shared(recv_sem, ext, 5, 0, -1)

    def slope(u, carry):
        zero = jnp.zeros((ROWS, CELLS), BF16)
        cols = []
        for i in range(2):
            column = ext[col_s[2 * u + i]]
            gathered[pl.ds(pl.multiple_of((2 * u + i) * ROWS, ROWS), ROWS), :] = column
            cols.append(column.astype(BF16))
        left = jnp.concatenate([jnp.concatenate([cols[0], zero], axis=1), jnp.concatenate([zero, cols[1]], axis=1)], axis=0)
        out = jnp.dot(left, jnp.concatenate([weights[2 * u], weights[2 * u + 1]], axis=0), preferred_element_type=F32)
        for i in range(2):
          for d in range(3):
            terms[pl.ds(pl.multiple_of(((2 * u + i) * 3 + d) * ROWS, ROWS), ROWS), :] = out[
                i * ROWS : (i + 1) * ROWS, d * CELLS : (d + 1) * CELLS
            ]
        return carry

    lax.fori_loop(0, TILES // 2, slope, 0, unroll=TILES // 2)

    def term(d, v):
        return terms[pl.ds(d * ROWS + v, TILES, stride=3 * ROWS), :]

    shear = [[term(d, 1 + i) for i in range(3)] for d in range(3)]
    third = (2.0 / 3.0) * (shear[0][0] + shear[1][1] + shear[2][2])
    sums = row_sums(
        owners,
        [
            2.0 * shear[0][0] - third,
            2.0 * shear[1][1] - third,
            shear[0][1] + shear[1][0],
            shear[0][2] + shear[2][0],
            shear[1][2] + shear[2][1],
        ]
        + [term(d, 4) for d in range(3)]
        + [term(d, 0) for d in range(3)],
    )
    rho, v0, v1, v2, press = [flat(ext)[pl.ds(v, PART, stride=ROWS), :] for v in range(5)]
    s00, s11, s01, s02, s12 = [0.3 * s for s in sums[:5]]
    s22 = -(s00 + s11)
    level = press / rho
    heat = [1.46 * (sums[5 + d] - level * sums[8 + d]) / rho for d in range(3)]
    work = [
        s00 * v0 + s01 * v1 + s02 * v2 + heat[0],
        s01 * v0 + s11 * v1 + s12 * v2 + heat[1],
        s02 * v0 + s12 * v1 + s22 * v2 + heat[2],
    ]
    for c, value in enumerate([s00, s01, s02, work[0], s11, s12, work[1], work[2]]):
        for s in range(SUBS):
            part_v[pl.ds((s * NUM_V + c) * OWN, OWN), :] = value[s * OWN : (s + 1) * OWN]

    def reduce_to_owners(part, recv, count, number):
        size = count * OWN
        for i, peer in enumerate(peers):
            remote(
                part.at[pl.ds(pl.multiple_of(peer * size, size), size)],
                recv.at[pl.ds(i * size, size)],
                number,
                (me, peer),
            )

    def reduced(part, recv, count, number):
        size = count * OWN
        drain(recv_sem, number, recv)
        total = part[pl.ds(pl.multiple_of(sub * size, size), size), :]
        for i in range(SUBS - 1):
            total = total + recv[pl.ds(i * size, size), :]
        return total

    size, part_rows = NUM_V * OWN, NUM_V * OWN // 2
    for half in range(2):
        for i, peer in enumerate(peers):
            remote(
                part_v.at[pl.ds(peer * size + half * part_rows, part_rows)],
                recv_v.at[pl.ds(i * size + half * part_rows, part_rows)],
                (10, 17)[half],
                (me, peer),
            )

    rho, v0, v1, v2, press = [gathered[pl.ds(v, TILES, stride=ROWS), :] for v in range(5)]
    vel = [v0, v1, v2]
    square = v0 * v0 + v1 * v1 + v2 * v2
    ener = 2.5 * press + 0.5 * rho * square
    wave = jnp.sqrt(square + 1.4 * press / rho)
    mom = [rho * v for v in vel]
    for v, value in enumerate([rho, *mom, ener]):
        scaled[pl.ds(v * TILES, TILES), :] = wave * value

    def dissipate(t, carry):
        left = scaled[pl.ds(t, ROWS, stride=TILES), :].astype(BF16)
        spread[pl.ds(pl.multiple_of(t * ROWS, ROWS), ROWS), :] = jnp.dot(
            left, absolute[t], preferred_element_type=F32
        )
        return carry

    lax.fori_loop(0, TILES, dissipate, 0, unroll=TILES)

    halves = [(own_v, packets_v, ext_v, 4, 5), (own_w, packets_w, ext_w, 4, 12)]
    for half, (mine, listed, extended, rows, first) in enumerate(halves):
        drain(recv_sem, (10, 17)[half], recv_v.at[pl.ds(0, (SUBS - 1) * part_rows)])
        total = part_v[pl.ds(sub * size + half * part_rows, part_rows), :]
        for i in range(SUBS - 1):
            total = total + recv_v[pl.ds(i * size + half * part_rows, part_rows), :]
        mixed[pl.ds(half * part_rows, part_rows), :] = total
        for r in range(OWN):
            mine[r, pl.ds(0, 4), :] = mixed[pl.ds(half * part_rows + r, 4, stride=OWN), :]
        share_lists(*halves[half], later)
    for mine, listed, extended, rows, first in halves:
        share_lists(mine, listed, extended, rows, first, earlier + same_chip)
        share_own(mine, extended, rows, first)

    def gather_v(t, carry):
        gathered_v[pl.ds(pl.multiple_of(t * ROWS, ROWS), ROWS), :] = ext_v[col_s[t]]
        return carry

    def gather_w(t, carry):
        gathered_w[pl.ds(pl.multiple_of(t * ROWS, ROWS), ROWS), :] = ext_w[col_s[t]]
        return carry

    for d in range(3):
        if d == 0:
            shared(recv_sem, ext_v, 4, 5, -1)
            lax.fori_loop(0, TILES, gather_v, 0, unroll=TILES)
            s00, s01, s02, w0 = [gathered_v[pl.ds(c, TILES, stride=ROWS), :] for c in range(4)]
            stress, work = [[s00, s01, s02]], [w0]
        if d == 1:

            def flux_first(t, carry):
                at = pl.multiple_of(t * ROWS, ROWS)
                left = fluxes[pl.ds(t, ROWS, stride=TILES), :].astype(BF16)
                total = jnp.dot(left, weights[t, :, pl.ds(0, CELLS)], preferred_element_type=F32)
                contribution[pl.ds(at, ROWS), :] = total - 0.1 * spread[pl.ds(at, ROWS), :]
                return carry

            lax.fori_loop(0, TILES, flux_first, 0, unroll=TILES)
            shared(recv_sem, ext_w, 4, 12, -1)
            lax.fori_loop(0, TILES, gather_w, 0, unroll=TILES)
            s11, s12, w1, w2 = [gathered_w[pl.ds(c, TILES, stride=ROWS), :] for c in range(4)]
            stress += [[s01, s11, s12], [s02, s12, -(s00 + s11)]]
            work += [w1, w2]
        values = [mom[d]]
        for i in range(3):
            flow = mom[i] * vel[d]
            if i == d:
                flow = flow + press
            values.append(flow - stress[d][i])
        values.append((ener + press) * vel[d] - work[d])
        for v, value in enumerate(values):
            fluxes[pl.ds((d * ROWS + v) * TILES, TILES), :] = value

    def flux(t, carry):
        at = pl.multiple_of(t * ROWS, ROWS)
        left = jnp.concatenate(
            [fluxes[pl.ds(d * ROWS * TILES + t, ROWS, stride=TILES), :] for d in (1, 2)],
            axis=1,
        ).astype(BF16)
        total = jnp.dot(
            left,
            jnp.concatenate([weights[t, :, pl.ds(d * CELLS, CELLS)] for d in (1, 2)], axis=0),
            preferred_element_type=F32,
        )
        contribution[pl.ds(at, ROWS), :] += total
        return carry

    lax.fori_loop(0, TILES, flux, 0, unroll=TILES)

    sums = row_sums(
        owners, [contribution[pl.ds(v, TILES, stride=ROWS), :] for v in range(NUM_R)]
    )
    for c, value in enumerate(sums):
        for s in range(SUBS):
            part_r[pl.ds((s * NUM_R + c) * OWN, OWN), :] = value[s * OWN : (s + 1) * OWN]
    reduce_to_owners(part_r, recv_r, NUM_R, 11)

    loads[1].wait()
    loads[2].wait()
    total = reduced(part_r, recv_r, NUM_R, 11)
    absolute_sum = total[5 * OWN : 6 * OWN] * speed
    half = 0.5 * ratio[...]
    for v, value in enumerate([density, *momentum, energy]):
        residual = total[v * OWN : (v + 1) * OWN] - absolute_sum * value
        out_ref[v] = base[v] - half * residual

    shared(send_sem, ext, 5, 0, 1)
    for number in (10, 17):
        drain(send_sem, number, recv_v.at[pl.ds(0, (SUBS - 1) * part_rows)])
    shared(send_sem, ext_v, 4, 5, 1)
    shared(send_sem, ext_w, 4, 12, 1)
    drain(send_sem, 11, recv_r)


def per_device(
    section_state, base_state, ratio, send_list, face_tiles, tile_row, tile_col, tile_flip
):
    any_space = pl.BlockSpec(memory_space=pl.ANY)
    scalars = lambda *shape: pltpu.SMEM(shape, jnp.int32)
    blocks = lambda count: pltpu.VMEM((count, ROWS, CELLS), F32)
    row = lambda count: pltpu.VMEM((count, CELLS), F32)
    updated = pl.pallas_call(
        functools.partial(kernel, lax.axis_size("dom")),
        out_shape=jax.ShapeDtypeStruct((5, OWN, CELLS), F32),
        in_specs=[any_space] * 8,
        out_specs=pl.BlockSpec(memory_space=pltpu.VMEM),
        scratch_shapes=[
            pltpu.VMEM((TILES, 3, CELLS, CELLS), BF16),
            pltpu.VMEM((TILES, CELLS, 3 * CELLS), BF16),
            pltpu.VMEM((TILES, CELLS, CELLS), BF16),
            pltpu.VMEM((5, OWN, CELLS), F32),
            pltpu.VMEM((5, OWN, CELLS), F32),
            pltpu.VMEM((OWN, CELLS), F32),
            blocks(OWN),
            blocks(len(CURVE_STEPS) * LIST),
            blocks(SLOTS),
            row(TILES * ROWS),
            row(TILES * 3 * ROWS),
            row(SUBS * NUM_V * OWN),
            row((SUBS - 1) * NUM_V * OWN),
            row(NUM_V * OWN),
            blocks(OWN),
            blocks(len(CURVE_STEPS) * LIST),
            blocks(SLOTS),
            row(TILES * ROWS),
            blocks(OWN),
            blocks(len(CURVE_STEPS) * LIST),
            blocks(SLOTS),
            row(TILES * ROWS),
            row(ROWS * TILES),
            row(TILES * ROWS),
            row(3 * ROWS * TILES),
            row(TILES * ROWS),
            row(SUBS * NUM_R * OWN),
            row((SUBS - 1) * NUM_R * OWN),
            scalars(*send_list.shape),
            scalars(TILES),
            scalars(TILES),
            scalars(TILES),
            pltpu.SemaphoreType.DMA((CHUNKS,)),
            pltpu.SemaphoreType.DMA((7,)),
            pltpu.SemaphoreType.DMA((18,)),
            pltpu.SemaphoreType.DMA((18,)),
        ],
        compiler_params=pltpu.CompilerParams(
            collective_id=0, has_side_effects=True, vmem_limit_bytes=60 * 1024 * 1024
        ),
    )(
        jnp.transpose(section_state, (1, 0, 2)),
        jnp.transpose(base_state, (1, 0, 2)),
        ratio,
        send_list,
        tile_row,
        tile_col,
        tile_flip,
        face_tiles,
    )
    return jnp.transpose(updated, (1, 0, 2))


def solution(mesh):
    return jax.shard_map(
        per_device,
        mesh=mesh,
        in_specs=(
            P(("dom", "sub"), None, None),
            P(("dom", "sub"), None, None),
            P(("dom", "sub"), None),
            P("dom", "sub", None, None),
            P(("dom", "sub"), None, None, None),
            P(("dom", "sub")),
            P(("dom", "sub")),
            P(("dom", "sub")),
        ),
        out_specs=P(("dom", "sub"), None, None),
        check_vma=False,
    )
```

```python
import functools

import jax
import jax.numpy as jnp
from jax import lax
from jax.experimental import pallas as pl
from jax.experimental.pallas import tpu as pltpu
from jax.sharding import PartitionSpec as P

MESH = pl.DeviceIdType.MESH
F32, BF16 = jnp.float32, jnp.bfloat16
CURVE_STEPS = (1, -1, 2, -2)
SUBS = 4
OWN = 8
PART = SUBS * OWN
LIST = 4
TILES = 32
CELLS = 128
SLOTS = PART + len(CURVE_STEPS) * SUBS * LIST
ROWS = 8
CHUNKS = 4
NUM_V = 8
NUM_R = 6


def row_sums(owners, parts):
    x = jnp.concatenate(parts, axis=1)
    high = x.astype(BF16)
    rest = x - high.astype(F32)
    mid = rest.astype(BF16)
    low = (rest - mid.astype(F32)).astype(BF16)
    total = jnp.dot(
        owners, jnp.concatenate([high, mid, low], axis=0), preferred_element_type=F32
    )
    return [total[:, i * CELLS : (i + 1) * CELLS] for i in range(len(parts))]


def kernel(
    doms,
    state_h,
    base_h,
    ratio_h,
    send_h,
    row_h,
    col_h,
    flip_h,
    tiles_h,
    out_ref,
    raw,
    weights,
    absolute,
    state,
    base,
    ratio,
    own,
    packets,
    ext,
    gathered,
    terms,
    part_v,
    recv_v,
    mixed,
    own_v,
    packets_v,
    ext_v,
    gathered_v,
    own_w,
    packets_w,
    ext_w,
    gathered_w,
    scaled,
    spread,
    fluxes,
    contribution,
    part_r,
    recv_r,
    send_s,
    row_s,
    col_s,
    flip_s,
    tile_sem,
    load_sem,
    send_sem,
    recv_sem,
):
    me, sub = lax.axis_index("dom"), lax.axis_index("sub")
    peers = [lax.rem(sub + i, SUBS) for i in (2, 1, 3)]
    targets = [me + step for step in CURVE_STEPS]
    inside = lambda dom: (dom >= 0) & (dom < doms)

    barrier = pltpu.get_barrier_semaphore()
    greeted = SUBS - 1
    for target in [targets[k] for k in (2, 0, 3, 1)]:
        greeted = greeted + jnp.where(inside(target), SUBS, 0)

        @pl.when(inside(target))
        def _():
            for s in range(SUBS):
                pl.semaphore_signal(
                    barrier, inc=1, device_id=(target, jnp.int32(s)), device_id_type=MESH
                )

    for peer in peers:
        pl.semaphore_signal(barrier, inc=1, device_id=(me, peer), device_id_type=MESH)

    loads = [
        pltpu.make_async_copy(state_h, state, load_sem.at[0]),
        pltpu.make_async_copy(base_h, base, load_sem.at[1]),
        pltpu.make_async_copy(ratio_h, ratio, load_sem.at[2]),
        pltpu.make_async_copy(send_h, send_s, load_sem.at[3]),
        pltpu.make_async_copy(row_h, row_s, load_sem.at[4]),
        pltpu.make_async_copy(col_h, col_s, load_sem.at[5]),
        pltpu.make_async_copy(flip_h, flip_s, load_sem.at[6]),
    ]
    for load in loads:
        load.start()
    per_chunk = TILES // CHUNKS
    tile_loads = [
        pltpu.make_async_copy(
            tiles_h.at[pl.ds(c * per_chunk, per_chunk)],
            raw.at[pl.ds(c * per_chunk, per_chunk)],
            tile_sem.at[c],
        )
        for c in range(CHUNKS)
    ]
    for load in tile_loads:
        load.start()

    def remote(source, target, number, device):
        pltpu.make_async_remote_copy(
            src_ref=source,
            dst_ref=target,
            send_sem=send_sem.at[number],
            recv_sem=recv_sem.at[number],
            device_id=device,
            device_id_type=MESH,
        ).start()

    def drain(sems, number, like):
        pltpu.make_async_copy(like, like, sems.at[number]).wait()

    core = lax.rem(me, 2)

    def pick(values, lists, k):
        for j in range(LIST):
            lists[k * LIST + j] = values[jnp.maximum(send_s[0, 0, k, j], 0)]

    def share_lists(values, lists, extended, rows, first, order, picked=False):
        def send(k):
            if not picked:
                pick(values, lists, k)
            for i in (2, 1, 3, 0):
                remote(
                    lists.at[pl.ds(k * LIST, LIST), pl.ds(0, rows)],
                    extended.at[pl.ds(PART + (k * SUBS + sub) * LIST, LIST), pl.ds(0, rows)],
                    first + k,
                    (targets[k], lax.rem(sub + i, SUBS)),
                )

        for k, where in order:
            pl.when(inside(targets[k]) & where)(functools.partial(send, k))

    def share_own(values, extended, rows, first):
        for peer in peers:
            remote(
                values.at[:, pl.ds(0, rows)],
                extended.at[pl.ds(sub * OWN, OWN), pl.ds(0, rows)],
                first + 4,
                (me, peer),
            )
        extended[pl.ds(sub * OWN, OWN)] = values[...]

    later = [(2, True), (0, core == 1)]
    earlier = [(3, True), (1, core == 0)]
    same_chip = [(0, core == 0), (1, core == 1)]

    def shared(sems, extended, rows, first, sign):
        for k, step in enumerate(CURVE_STEPS):

            @pl.when(inside(me + sign * step))
            def _():
                drain(sems, first + k, extended.at[pl.ds(0, SUBS * LIST), pl.ds(0, rows)])

        drain(sems, first + 4, extended.at[pl.ds(0, PART - OWN), pl.ds(0, rows)])

    flat = lambda ref: ref.reshape(ref.shape[0] * ROWS, CELLS)

    loads[0].wait()
    loads[3].wait()
    density, energy = state[0], state[4]
    momentum = [state[1 + i] for i in range(3)]
    velocity = [m / density for m in momentum]
    pressure = 0.4 * (
        energy
        - 0.5
        * (momentum[0] * velocity[0] + momentum[1] * velocity[1] + momentum[2] * velocity[2])
    )
    square = velocity[0] * velocity[0] + velocity[1] * velocity[1] + velocity[2] * velocity[2]
    speed = jnp.sqrt(square + 1.4 * pressure / density)
    for i, value in enumerate(
        [density, *velocity, pressure]
    ):
        flat(own)[pl.ds(i, OWN, stride=ROWS), :] = value

    for k in range(len(CURVE_STEPS)):
        pick(own, packets, k)

    pl.semaphore_wait(barrier, greeted)
    share_lists(own, packets, ext, 5, 0, earlier + later + same_chip, picked=True)
    share_own(own, ext, 5, 0)

    for load in loads[4:]:
        load.wait()
    lane = lax.broadcasted_iota(jnp.int32, (PART, 3 * TILES), 1)
    lane = lax.rem(lane, TILES)
    tile_rows = jnp.zeros((PART, 3 * TILES), jnp.int32)
    for t in range(TILES):
        tile_rows = jnp.where(lane == t, row_s[t], tile_rows)
    block_row = lax.broadcasted_iota(jnp.int32, (PART, 3 * TILES), 0)
    owners = jnp.where(block_row == tile_rows, 1.0, 0.0).astype(BF16)

    def orient(t, carry):
        flipped = jnp.full((CELLS, CELLS), flip_s[t], jnp.int32) == 1
        total = None
        for d in range(3):
            tile = raw[t, d].astype(F32)
            tile = jnp.where(flipped, -tile, tile.T)
            weights[t, :, pl.ds(d * CELLS, CELLS)] = tile.astype(BF16)
            total = jnp.abs(tile) if total is None else total + jnp.abs(tile)
        absolute[t] = total.astype(BF16)
        return carry

    for c in range(CHUNKS):
        tile_loads[c].wait()
        lax.fori_loop(c * per_chunk, (c + 1) * per_chunk, orient, 0)
    ones = jnp.ones((TILES, CELLS), F32)
    scaled[pl.ds(5 * TILES, TILES), :] = ones
    for v in (6, 7):
        scaled[pl.ds(v * TILES, TILES), :] = jnp.zeros_like(ones)
    for d in range(3):
        for v in (5, 6, 7):
            fluxes[pl.ds((d * ROWS + v) * TILES, TILES), :] = jnp.zeros_like(ones)

    shared(recv_sem, ext, 5, 0, -1)

    def slope(u, carry):
        zero = jnp.zeros((ROWS, CELLS), BF16)
        cols = []
        for i in range(2):
            column = ext[col_s[2 * u + i]]
            gathered[pl.ds(pl.multiple_of((2 * u + i) * ROWS, ROWS), ROWS), :] = column
            cols.append(column.astype(BF16))
        left = jnp.concatenate([jnp.concatenate([cols[0], zero], axis=1), jnp.concatenate([zero, cols[1]], axis=1)], axis=0)
        out = jnp.dot(left, jnp.concatenate([weights[2 * u], weights[2 * u + 1]], axis=0), preferred_element_type=F32)
        for i in range(2):
          for d in range(3):
            terms[pl.ds(pl.multiple_of(((2 * u + i) * 3 + d) * ROWS, ROWS), ROWS), :] = out[
                i * ROWS : (i + 1) * ROWS, d * CELLS : (d + 1) * CELLS
            ]
        return carry

    lax.fori_loop(0, TILES // 2, slope, 0, unroll=TILES // 2)

    def term(d, v):
        return terms[pl.ds(d * ROWS + v, TILES, stride=3 * ROWS), :]

    shear = [[term(d, 1 + i) for i in range(3)] for d in range(3)]
    third = (2.0 / 3.0) * (shear[0][0] + shear[1][1] + shear[2][2])
    sums = row_sums(
        owners,
        [
            2.0 * shear[0][0] - third,
            2.0 * shear[1][1] - third,
            shear[0][1] + shear[1][0],
            shear[0][2] + shear[2][0],
            shear[1][2] + shear[2][1],
        ]
        + [term(d, 4) for d in range(3)]
        + [term(d, 0) for d in range(3)],
    )
    rho, v0, v1, v2, press = [flat(ext)[pl.ds(v, PART, stride=ROWS), :] for v in range(5)]
    s00, s11, s01, s02, s12 = [0.3 * s for s in sums[:5]]
    s22 = -(s00 + s11)
    level = press / rho
    heat = [1.46 * (sums[5 + d] - level * sums[8 + d]) / rho for d in range(3)]
    work = [
        s00 * v0 + s01 * v1 + s02 * v2 + heat[0],
        s01 * v0 + s11 * v1 + s12 * v2 + heat[1],
        s02 * v0 + s12 * v1 + s22 * v2 + heat[2],
    ]
    for c, value in enumerate([s00, s01, s02, work[0], s11, s12, work[1], work[2]]):
        for s in range(SUBS):
            part_v[pl.ds((s * NUM_V + c) * OWN, OWN), :] = value[s * OWN : (s + 1) * OWN]

    def reduce_to_owners(part, recv, count, number):
        size = count * OWN
        for i, peer in enumerate(peers):
            remote(
                part.at[pl.ds(pl.multiple_of(peer * size, size), size)],
                recv.at[pl.ds(i * size, size)],
                number,
                (me, peer),
            )

    def reduced(part, recv, count, number):
        size = count * OWN
        drain(recv_sem, number, recv)
        total = part[pl.ds(pl.multiple_of(sub * size, size), size), :]
        for i in range(SUBS - 1):
            total = total + recv[pl.ds(i * size, size), :]
        return total

    size, part_rows = NUM_V * OWN, NUM_V * OWN // 2
    for half in range(2):
        for i, peer in enumerate(peers):
            remote(
                part_v.at[pl.ds(peer * size + half * part_rows, part_rows)],
                recv_v.at[pl.ds(i * size + half * part_rows, part_rows)],
                (10, 17)[half],
                (me, peer),
            )

    rho, v0, v1, v2, press = [gathered[pl.ds(v, TILES, stride=ROWS), :] for v in range(5)]
    vel = [v0, v1, v2]
    square = v0 * v0 + v1 * v1 + v2 * v2
    ener = 2.5 * press + 0.5 * rho * square
    wave = jnp.sqrt(square + 1.4 * press / rho)
    mom = [rho * v for v in vel]
    for v, value in enumerate([rho, *mom, ener]):
        scaled[pl.ds(v * TILES, TILES), :] = wave * value

    def dissipate(t, carry):
        left = scaled[pl.ds(t, ROWS, stride=TILES), :].astype(BF16)
        spread[pl.ds(pl.multiple_of(t * ROWS, ROWS), ROWS), :] = jnp.dot(
            left, absolute[t], preferred_element_type=F32
        )
        return carry

    lax.fori_loop(0, TILES, dissipate, 0, unroll=TILES)

    halves = [(own_v, packets_v, ext_v, 4, 5), (own_w, packets_w, ext_w, 4, 12)]
    for half, (mine, listed, extended, rows, first) in enumerate(halves):
        drain(recv_sem, (10, 17)[half], recv_v.at[pl.ds(0, (SUBS - 1) * part_rows)])
        total = part_v[pl.ds(sub * size + half * part_rows, part_rows), :]
        for i in range(SUBS - 1):
            total = total + recv_v[pl.ds(i * size + half * part_rows, part_rows), :]
        mixed[pl.ds(half * part_rows, part_rows), :] = total
        for r in range(OWN):
            mine[r, pl.ds(0, 4), :] = mixed[pl.ds(half * part_rows + r, 4, stride=OWN), :]
        share_lists(*halves[half], later)
    for mine, listed, extended, rows, first in halves:
        share_lists(mine, listed, extended, rows, first, earlier + same_chip)
        share_own(mine, extended, rows, first)

    def gather_v(t, carry):
        gathered_v[pl.ds(pl.multiple_of(t * ROWS, ROWS), ROWS), :] = ext_v[col_s[t]]
        return carry

    def gather_w(t, carry):
        gathered_w[pl.ds(pl.multiple_of(t * ROWS, ROWS), ROWS), :] = ext_w[col_s[t]]
        return carry

    for d in range(3):
        if d == 0:
            shared(recv_sem, ext_v, 4, 5, -1)
            lax.fori_loop(0, TILES, gather_v, 0, unroll=TILES)
            s00, s01, s02, w0 = [gathered_v[pl.ds(c, TILES, stride=ROWS), :] for c in range(4)]
            stress, work = [[s00, s01, s02]], [w0]
        if d == 1:

            def flux_first(t, carry):
                at = pl.multiple_of(t * ROWS, ROWS)
                left = fluxes[pl.ds(t, ROWS, stride=TILES), :].astype(BF16)
                total = jnp.dot(left, weights[t, :, pl.ds(0, CELLS)], preferred_element_type=F32)
                contribution[pl.ds(at, ROWS), :] = total - 0.1 * spread[pl.ds(at, ROWS), :]
                return carry

            lax.fori_loop(0, TILES, flux_first, 0, unroll=TILES)
            shared(recv_sem, ext_w, 4, 12, -1)
            lax.fori_loop(0, TILES, gather_w, 0, unroll=TILES)
            s11, s12, w1, w2 = [gathered_w[pl.ds(c, TILES, stride=ROWS), :] for c in range(4)]
            stress += [[s01, s11, s12], [s02, s12, -(s00 + s11)]]
            work += [w1, w2]
        values = [mom[d]]
        for i in range(3):
            flow = mom[i] * vel[d]
            if i == d:
                flow = flow + press
            values.append(flow - stress[d][i])
        values.append((ener + press) * vel[d] - work[d])
        for v, value in enumerate(values):
            fluxes[pl.ds((d * ROWS + v) * TILES, TILES), :] = value

    def flux(t, carry):
        at = pl.multiple_of(t * ROWS, ROWS)
        left = jnp.concatenate(
            [fluxes[pl.ds(d * ROWS * TILES + t, ROWS, stride=TILES), :] for d in (1, 2)],
            axis=1,
        ).astype(BF16)
        total = jnp.dot(
            left,
            jnp.concatenate([weights[t, :, pl.ds(d * CELLS, CELLS)] for d in (1, 2)], axis=0),
            preferred_element_type=F32,
        )
        contribution[pl.ds(at, ROWS), :] += total
        return carry

    lax.fori_loop(0, TILES, flux, 0, unroll=TILES)

    sums = row_sums(
        owners, [contribution[pl.ds(v, TILES, stride=ROWS), :] for v in range(NUM_R)]
    )
    for c, value in enumerate(sums):
        for s in range(SUBS):
            part_r[pl.ds((s * NUM_R + c) * OWN, OWN), :] = value[s * OWN : (s + 1) * OWN]
    reduce_to_owners(part_r, recv_r, NUM_R, 11)

    loads[1].wait()
    loads[2].wait()
    total = reduced(part_r, recv_r, NUM_R, 11)
    absolute_sum = total[5 * OWN : 6 * OWN] * speed
    half = 0.5 * ratio[...]
    for v, value in enumerate([density, *momentum, energy]):
        residual = total[v * OWN : (v + 1) * OWN] - absolute_sum * value
        out_ref[v] = base[v] - half * residual

    shared(send_sem, ext, 5, 0, 1)
    for number in (10, 17):
        drain(send_sem, number, recv_v.at[pl.ds(0, (SUBS - 1) * part_rows)])
    shared(send_sem, ext_v, 4, 5, 1)
    shared(send_sem, ext_w, 4, 12, 1)
    drain(send_sem, 11, recv_r)


def per_device(
    section_state, base_state, ratio, send_list, face_tiles, tile_row, tile_col, tile_flip
):
    any_space = pl.BlockSpec(memory_space=pl.ANY)
    scalars = lambda *shape: pltpu.SMEM(shape, jnp.int32)
    blocks = lambda count: pltpu.VMEM((count, ROWS, CELLS), F32)
    row = lambda count: pltpu.VMEM((count, CELLS), F32)
    updated = pl.pallas_call(
        functools.partial(kernel, lax.axis_size("dom")),
        out_shape=jax.ShapeDtypeStruct((5, OWN, CELLS), F32),
        in_specs=[any_space] * 8,
        out_specs=pl.BlockSpec(memory_space=pltpu.VMEM),
        scratch_shapes=[
            pltpu.VMEM((TILES, 3, CELLS, CELLS), BF16),
            pltpu.VMEM((TILES, CELLS, 3 * CELLS), BF16),
            pltpu.VMEM((TILES, CELLS, CELLS), BF16),
            pltpu.VMEM((5, OWN, CELLS), F32),
            pltpu.VMEM((5, OWN, CELLS), F32),
            pltpu.VMEM((OWN, CELLS), F32),
            blocks(OWN),
            blocks(len(CURVE_STEPS) * LIST),
            blocks(SLOTS),
            row(TILES * ROWS),
            row(TILES * 3 * ROWS),
            row(SUBS * NUM_V * OWN),
            row((SUBS - 1) * NUM_V * OWN),
            row(NUM_V * OWN),
            blocks(OWN),
            blocks(len(CURVE_STEPS) * LIST),
            blocks(SLOTS),
            row(TILES * ROWS),
            blocks(OWN),
            blocks(len(CURVE_STEPS) * LIST),
            blocks(SLOTS),
            row(TILES * ROWS),
            row(ROWS * TILES),
            row(TILES * ROWS),
            row(3 * ROWS * TILES),
            row(TILES * ROWS),
            row(SUBS * NUM_R * OWN),
            row((SUBS - 1) * NUM_R * OWN),
            scalars(*send_list.shape),
            scalars(TILES),
            scalars(TILES),
            scalars(TILES),
            pltpu.SemaphoreType.DMA((CHUNKS,)),
            pltpu.SemaphoreType.DMA((7,)),
            pltpu.SemaphoreType.DMA((18,)),
            pltpu.SemaphoreType.DMA((18,)),
        ],
        compiler_params=pltpu.CompilerParams(
            collective_id=0, has_side_effects=True, vmem_limit_bytes=60 * 1024 * 1024
        ),
    )(
        jnp.transpose(section_state, (1, 0, 2)),
        jnp.transpose(base_state, (1, 0, 2)),
        ratio,
        send_list,
        tile_row,
        tile_col,
        tile_flip,
        face_tiles,
    )
    return jnp.transpose(updated, (1, 0, 2))


def solution(mesh):
    return jax.shard_map(
        per_device,
        mesh=mesh,
        in_specs=(
            P(("dom", "sub"), None, None),
            P(("dom", "sub"), None, None),
            P(("dom", "sub"), None),
            P("dom", "sub", None, None),
            P(("dom", "sub"), None, None, None),
            P(("dom", "sub")),
            P(("dom", "sub")),
            P(("dom", "sub")),
        ),
        out_specs=P(("dom", "sub"), None, None),
        check_vma=False,
    )
```

```python
import functools

import jax
import jax.numpy as jnp
from jax import lax
from jax.experimental import pallas as pl
from jax.experimental.pallas import tpu as pltpu
from jax.sharding import PartitionSpec as P

MESH = pl.DeviceIdType.MESH
F32, BF16 = jnp.float32, jnp.bfloat16
CURVE_STEPS = (1, -1, 2, -2)
SUBS = 4
OWN = 8
PART = SUBS * OWN
LIST = 4
TILES = 32
CELLS = 128
SLOTS = PART + len(CURVE_STEPS) * SUBS * LIST
ROWS = 8
CHUNKS = 4
NUM_V = 8
NUM_R = 6


def row_sums(owners, parts):
    x = jnp.concatenate(parts, axis=1)
    high = x.astype(BF16)
    rest = x - high.astype(F32)
    mid = rest.astype(BF16)
    low = (rest - mid.astype(F32)).astype(BF16)
    total = jnp.dot(
        owners, jnp.concatenate([high, mid, low], axis=0), preferred_element_type=F32
    )
    return [total[:, i * CELLS : (i + 1) * CELLS] for i in range(len(parts))]


def kernel(
    doms,
    state_h,
    base_h,
    ratio_h,
    send_h,
    row_h,
    col_h,
    flip_h,
    tiles_h,
    out_ref,
    raw,
    weights,
    absolute,
    state,
    base,
    ratio,
    own,
    packets,
    ext,
    gathered,
    terms,
    part_v,
    recv_v,
    mixed,
    own_v,
    packets_v,
    ext_v,
    gathered_v,
    scaled,
    spread,
    fluxes,
    contribution,
    part_r,
    recv_r,
    send_s,
    row_s,
    col_s,
    flip_s,
    tile_sem,
    load_sem,
    send_sem,
    recv_sem,
):
    me, sub = lax.axis_index("dom"), lax.axis_index("sub")
    peers = [lax.rem(sub + i, SUBS) for i in (2, 1, 3)]
    targets = [me + step for step in CURVE_STEPS]
    inside = lambda dom: (dom >= 0) & (dom < doms)

    barrier = pltpu.get_barrier_semaphore()
    greeted = SUBS - 1
    for target in [targets[k] for k in (2, 0, 3, 1)]:
        greeted = greeted + jnp.where(inside(target), SUBS, 0)

        @pl.when(inside(target))
        def _():
            for s in range(SUBS):
                pl.semaphore_signal(
                    barrier, inc=1, device_id=(target, jnp.int32(s)), device_id_type=MESH
                )

    for peer in peers:
        pl.semaphore_signal(barrier, inc=1, device_id=(me, peer), device_id_type=MESH)

    loads = [
        pltpu.make_async_copy(state_h, state, load_sem.at[0]),
        pltpu.make_async_copy(base_h, base, load_sem.at[1]),
        pltpu.make_async_copy(ratio_h, ratio, load_sem.at[2]),
        pltpu.make_async_copy(send_h, send_s, load_sem.at[3]),
        pltpu.make_async_copy(row_h, row_s, load_sem.at[4]),
        pltpu.make_async_copy(col_h, col_s, load_sem.at[5]),
        pltpu.make_async_copy(flip_h, flip_s, load_sem.at[6]),
    ]
    for load in loads:
        load.start()
    per_chunk = TILES // CHUNKS
    tile_loads = [
        pltpu.make_async_copy(
            tiles_h.at[pl.ds(c * per_chunk, per_chunk)],
            raw.at[pl.ds(c * per_chunk, per_chunk)],
            tile_sem.at[c],
        )
        for c in range(CHUNKS)
    ]
    for load in tile_loads:
        load.start()

    def remote(source, target, number, device):
        pltpu.make_async_remote_copy(
            src_ref=source,
            dst_ref=target,
            send_sem=send_sem.at[number],
            recv_sem=recv_sem.at[number],
            device_id=device,
            device_id_type=MESH,
        ).start()

    def drain(sems, number, like):
        pltpu.make_async_copy(like, like, sems.at[number]).wait()

    core = lax.rem(me, 2)

    def pick(values, lists, k):
        for j in range(LIST):
            lists[k * LIST + j] = values[jnp.maximum(send_s[0, 0, k, j], 0)]

    def share_lists(values, lists, extended, rows, first, order, picked=False):
        def send(k):
            if not picked:
                pick(values, lists, k)
            for i in (2, 1, 3, 0):
                remote(
                    lists.at[pl.ds(k * LIST, LIST), pl.ds(0, rows)],
                    extended.at[pl.ds(PART + (k * SUBS + sub) * LIST, LIST), pl.ds(0, rows)],
                    first + k,
                    (targets[k], lax.rem(sub + i, SUBS)),
                )

        for k, where in order:
            pl.when(inside(targets[k]) & where)(functools.partial(send, k))

    def share_own(values, extended, rows, first):
        for peer in peers:
            remote(
                values.at[:, pl.ds(0, rows)],
                extended.at[pl.ds(sub * OWN, OWN), pl.ds(0, rows)],
                first + 4,
                (me, peer),
            )
        extended[pl.ds(sub * OWN, OWN)] = values[...]

    later = [(2, True), (0, core == 1)]
    earlier = [(3, True), (1, core == 0)]
    same_chip = [(0, core == 0), (1, core == 1)]

    def shared(sems, extended, rows, first, sign):
        for k, step in enumerate(CURVE_STEPS):

            @pl.when(inside(me + sign * step))
            def _():
                drain(sems, first + k, extended.at[pl.ds(0, SUBS * LIST), pl.ds(0, rows)])

        drain(sems, first + 4, extended.at[pl.ds(0, PART - OWN), pl.ds(0, rows)])

    flat = lambda ref: ref.reshape(ref.shape[0] * ROWS, CELLS)

    loads[0].wait()
    loads[3].wait()
    density, energy = state[0], state[4]
    momentum = [state[1 + i] for i in range(3)]
    velocity = [m / density for m in momentum]
    pressure = 0.4 * (
        energy
        - 0.5
        * (momentum[0] * velocity[0] + momentum[1] * velocity[1] + momentum[2] * velocity[2])
    )
    square = velocity[0] * velocity[0] + velocity[1] * velocity[1] + velocity[2] * velocity[2]
    speed = jnp.sqrt(square + 1.4 * pressure / density)
    for i, value in enumerate(
        [density, *velocity, pressure]
    ):
        flat(own)[pl.ds(i, OWN, stride=ROWS), :] = value

    for k in range(len(CURVE_STEPS)):
        pick(own, packets, k)

    pl.semaphore_wait(barrier, greeted)
    share_lists(own, packets, ext, 5, 0, earlier + later + same_chip, picked=True)
    share_own(own, ext, 5, 0)

    for load in loads[4:]:
        load.wait()
    lane = lax.broadcasted_iota(jnp.int32, (PART, 3 * TILES), 1)
    lane = lax.rem(lane, TILES)
    tile_rows = jnp.zeros((PART, 3 * TILES), jnp.int32)
    for t in range(TILES):
        tile_rows = jnp.where(lane == t, row_s[t], tile_rows)
    block_row = lax.broadcasted_iota(jnp.int32, (PART, 3 * TILES), 0)
    owners = jnp.where(block_row == tile_rows, 1.0, 0.0).astype(BF16)

    def orient(t, carry):
        flipped = jnp.full((CELLS, CELLS), flip_s[t], jnp.int32) == 1
        total = None
        for d in range(3):
            tile = raw[t, d].astype(F32)
            tile = jnp.where(flipped, -tile, tile.T)
            weights[t, :, pl.ds(d * CELLS, CELLS)] = tile.astype(BF16)
            total = jnp.abs(tile) if total is None else total + jnp.abs(tile)
        absolute[t] = total.astype(BF16)
        return carry

    for c in range(CHUNKS):
        tile_loads[c].wait()
        lax.fori_loop(c * per_chunk, (c + 1) * per_chunk, orient, 0)
    ones = jnp.ones((TILES, CELLS), F32)
    scaled[pl.ds(5 * TILES, TILES), :] = ones
    for v in (6, 7):
        scaled[pl.ds(v * TILES, TILES), :] = jnp.zeros_like(ones)
    for d in range(3):
        for v in (5, 6, 7):
            fluxes[pl.ds((d * ROWS + v) * TILES, TILES), :] = jnp.zeros_like(ones)

    shared(recv_sem, ext, 5, 0, -1)

    def slope(u, carry):
        zero = jnp.zeros((ROWS, CELLS), BF16)
        cols = []
        for i in range(2):
            column = ext[col_s[2 * u + i]]
            gathered[pl.ds(pl.multiple_of((2 * u + i) * ROWS, ROWS), ROWS), :] = column
            cols.append(column.astype(BF16))
        left = jnp.concatenate([jnp.concatenate([cols[0], zero], axis=1), jnp.concatenate([zero, cols[1]], axis=1)], axis=0)
        out = jnp.dot(left, jnp.concatenate([weights[2 * u], weights[2 * u + 1]], axis=0), preferred_element_type=F32)
        for i in range(2):
          for d in range(3):
            terms[pl.ds(pl.multiple_of(((2 * u + i) * 3 + d) * ROWS, ROWS), ROWS), :] = out[
                i * ROWS : (i + 1) * ROWS, d * CELLS : (d + 1) * CELLS
            ]
        return carry

    lax.fori_loop(0, TILES // 2, slope, 0, unroll=TILES // 2)

    def term(d, v):
        return terms[pl.ds(d * ROWS + v, TILES, stride=3 * ROWS), :]

    shear = [[term(d, 1 + i) for i in range(3)] for d in range(3)]
    third = (2.0 / 3.0) * (shear[0][0] + shear[1][1] + shear[2][2])
    sums = row_sums(
        owners,
        [
            2.0 * shear[0][0] - third,
            2.0 * shear[1][1] - third,
            shear[0][1] + shear[1][0],
            shear[0][2] + shear[2][0],
            shear[1][2] + shear[2][1],
        ]
        + [term(d, 4) for d in range(3)]
        + [term(d, 0) for d in range(3)],
    )
    rho, v0, v1, v2, press = [flat(ext)[pl.ds(v, PART, stride=ROWS), :] for v in range(5)]
    s00, s11, s01, s02, s12 = [0.3 * s for s in sums[:5]]
    s22 = -(s00 + s11)
    level = press / rho
    heat = [1.46 * (sums[5 + d] - level * sums[8 + d]) / rho for d in range(3)]
    work = [
        s00 * v0 + s01 * v1 + s02 * v2 + heat[0],
        s01 * v0 + s11 * v1 + s12 * v2 + heat[1],
        s02 * v0 + s12 * v1 + s22 * v2 + heat[2],
    ]
    for c, value in enumerate([s00, s11, s01, s02, s12, *work]):
        for s in range(SUBS):
            part_v[pl.ds((s * NUM_V + c) * OWN, OWN), :] = value[s * OWN : (s + 1) * OWN]

    def reduce_to_owners(part, recv, count, number):
        size = count * OWN
        for i, peer in enumerate(peers):
            remote(
                part.at[pl.ds(pl.multiple_of(peer * size, size), size)],
                recv.at[pl.ds(i * size, size)],
                number,
                (me, peer),
            )

    def reduced(part, recv, count, number):
        size = count * OWN
        drain(recv_sem, number, recv)
        total = part[pl.ds(pl.multiple_of(sub * size, size), size), :]
        for i in range(SUBS - 1):
            total = total + recv[pl.ds(i * size, size), :]
        return total

    reduce_to_owners(part_v, recv_v, NUM_V, 10)

    rho, v0, v1, v2, press = [gathered[pl.ds(v, TILES, stride=ROWS), :] for v in range(5)]
    vel = [v0, v1, v2]
    square = v0 * v0 + v1 * v1 + v2 * v2
    ener = 2.5 * press + 0.5 * rho * square
    wave = jnp.sqrt(square + 1.4 * press / rho)
    mom = [rho * v for v in vel]
    for v, value in enumerate([rho, *mom, ener]):
        scaled[pl.ds(v * TILES, TILES), :] = wave * value

    def dissipate(t, carry):
        left = scaled[pl.ds(t, ROWS, stride=TILES), :].astype(BF16)
        spread[pl.ds(pl.multiple_of(t * ROWS, ROWS), ROWS), :] = jnp.dot(
            left, absolute[t], preferred_element_type=F32
        )
        return carry

    lax.fori_loop(0, TILES, dissipate, 0, unroll=TILES)

    mixed[...] = reduced(part_v, recv_v, NUM_V, 10)
    for r in range(OWN):
        own_v[r] = mixed[pl.ds(r, ROWS, stride=OWN), :]
    share_lists(own_v, packets_v, ext_v, ROWS, 5, later + earlier + same_chip)
    share_own(own_v, ext_v, ROWS, 5)
    shared(recv_sem, ext_v, ROWS, 5, -1)

    def gather_v(t, carry):
        gathered_v[pl.ds(pl.multiple_of(t * ROWS, ROWS), ROWS), :] = ext_v[col_s[t]]
        return carry

    lax.fori_loop(0, TILES, gather_v, 0, unroll=TILES)
    s00, s11, s01, s02, s12, w0, w1, w2 = [
        gathered_v[pl.ds(c, TILES, stride=ROWS), :] for c in range(NUM_V)
    ]
    stress = [[s00, s01, s02], [s01, s11, s12], [s02, s12, -(s00 + s11)]]
    work = [w0, w1, w2]
    for d in range(3):
        values = [mom[d]]
        for i in range(3):
            flow = mom[i] * vel[d]
            if i == d:
                flow = flow + press
            values.append(flow - stress[d][i])
        values.append((ener + press) * vel[d] - work[d])
        for v, value in enumerate(values):
            fluxes[pl.ds((d * ROWS + v) * TILES, TILES), :] = value

    def flux(t, carry):
        at = pl.multiple_of(t * ROWS, ROWS)
        left = jnp.concatenate(
            [fluxes[pl.ds(d * ROWS * TILES + t, ROWS, stride=TILES), :] for d in range(3)],
            axis=1,
        ).astype(BF16)
        total = jnp.dot(
            left,
            jnp.concatenate([weights[t, :, pl.ds(d * CELLS, CELLS)] for d in range(3)], axis=0),
            preferred_element_type=F32,
        )
        contribution[pl.ds(at, ROWS), :] = total - 0.1 * spread[pl.ds(at, ROWS), :]
        return carry

    lax.fori_loop(0, TILES, flux, 0, unroll=TILES)

    sums = row_sums(
        owners, [contribution[pl.ds(v, TILES, stride=ROWS), :] for v in range(NUM_R)]
    )
    for c, value in enumerate(sums):
        for s in range(SUBS):
            part_r[pl.ds((s * NUM_R + c) * OWN, OWN), :] = value[s * OWN : (s + 1) * OWN]
    reduce_to_owners(part_r, recv_r, NUM_R, 11)

    loads[1].wait()
    loads[2].wait()
    total = reduced(part_r, recv_r, NUM_R, 11)
    absolute_sum = total[5 * OWN : 6 * OWN] * speed
    half = 0.5 * ratio[...]
    for v, value in enumerate([density, *momentum, energy]):
        residual = total[v * OWN : (v + 1) * OWN] - absolute_sum * value
        out_ref[v] = base[v] - half * residual

    shared(send_sem, ext, 5, 0, 1)
    drain(send_sem, 10, recv_v)
    shared(send_sem, ext_v, ROWS, 5, 1)
    drain(send_sem, 11, recv_r)


def per_device(
    section_state, base_state, ratio, send_list, face_tiles, tile_row, tile_col, tile_flip
):
    any_space = pl.BlockSpec(memory_space=pl.ANY)
    scalars = lambda *shape: pltpu.SMEM(shape, jnp.int32)
    blocks = lambda count: pltpu.VMEM((count, ROWS, CELLS), F32)
    row = lambda count: pltpu.VMEM((count, CELLS), F32)
    updated = pl.pallas_call(
        functools.partial(kernel, lax.axis_size("dom")),
        out_shape=jax.ShapeDtypeStruct((5, OWN, CELLS), F32),
        in_specs=[any_space] * 8,
        out_specs=pl.BlockSpec(memory_space=pltpu.VMEM),
        scratch_shapes=[
            pltpu.VMEM((TILES, 3, CELLS, CELLS), BF16),
            pltpu.VMEM((TILES, CELLS, 3 * CELLS), BF16),
            pltpu.VMEM((TILES, CELLS, CELLS), BF16),
            pltpu.VMEM((5, OWN, CELLS), F32),
            pltpu.VMEM((5, OWN, CELLS), F32),
            pltpu.VMEM((OWN, CELLS), F32),
            blocks(OWN),
            blocks(len(CURVE_STEPS) * LIST),
            blocks(SLOTS),
            row(TILES * ROWS),
            row(TILES * 3 * ROWS),
            row(SUBS * NUM_V * OWN),
            row((SUBS - 1) * NUM_V * OWN),
            row(NUM_V * OWN),
            blocks(OWN),
            blocks(len(CURVE_STEPS) * LIST),
            blocks(SLOTS),
            row(TILES * ROWS),
            row(ROWS * TILES),
            row(TILES * ROWS),
            row(3 * ROWS * TILES),
            row(TILES * ROWS),
            row(SUBS * NUM_R * OWN),
            row((SUBS - 1) * NUM_R * OWN),
            scalars(*send_list.shape),
            scalars(TILES),
            scalars(TILES),
            scalars(TILES),
            pltpu.SemaphoreType.DMA((CHUNKS,)),
            pltpu.SemaphoreType.DMA((7,)),
            pltpu.SemaphoreType.DMA((12,)),
            pltpu.SemaphoreType.DMA((12,)),
        ],
        compiler_params=pltpu.CompilerParams(
            collective_id=0, has_side_effects=True, vmem_limit_bytes=60 * 1024 * 1024
        ),
    )(
        jnp.transpose(section_state, (1, 0, 2)),
        jnp.transpose(base_state, (1, 0, 2)),
        ratio,
        send_list,
        tile_row,
        tile_col,
        tile_flip,
        face_tiles,
    )
    return jnp.transpose(updated, (1, 0, 2))


def solution(mesh):
    return jax.shard_map(
        per_device,
        mesh=mesh,
        in_specs=(
            P(("dom", "sub"), None, None),
            P(("dom", "sub"), None, None),
            P(("dom", "sub"), None),
            P("dom", "sub", None, None),
            P(("dom", "sub"), None, None, None),
            P(("dom", "sub")),
            P(("dom", "sub")),
            P(("dom", "sub")),
        ),
        out_specs=P(("dom", "sub"), None, None),
        check_vma=False,
    )
```
